128 devices in a mesh: row: 16 (over x, z), col: 8 (over y, core).
Axes of the slice: x: 4, y: 4, z: 4, core: 2. Of those that a mesh axis runs over, the one named last changes fastest.
Arguments:
- partials: float32 [8, 8, 16, 1024, 128], P('col', None, 'row'), may hold values from -5 to 5
- panel: float32 [8, 16, 1024, 2, 1024], P(None, 'row', None, None, 'col'), may hold values from -0.1875 to 0.1875
- inverse: float32 [2, 1024, 1024], P(None, 'col'), as said below
- rhs_blocks: float32 [2, 1024, 128], replicated, may hold values from -6 to 6
Outputs:
- new_partials: float32 [8, 8, 16, 1024, 128], P('col', None, 'row')
- solved: float32 [2, 1024, 128], P(None, 'col')
The draws below stay inside these ranges and needn't reach their ends.
Inputs may be any that keep to these rules, and one draw needn't show every extreme that they name: `inverse`: each of the two blocks is lower triangular with a positive diagonal.
All inputs are finite; a program needn't handle non-finite values.
Results may differ from the reference program's by a relative error of at most 0.0001.
Values sent between devices are 32-bit elements; how exact they have to be, the bound alone decides.
No kernel may reach another device: no remote copies, remote signals or barrier semaphores. Data moves between devices by JAX's collectives and lax.ppermute only.
A program may use at most 128 MiB of HBM per device.

```python
import math
import jax
import jax.numpy as jnp
from jax import lax

NB = 1024
RHS = 128
BR_DEV = 8
N_ROW = 16
N_COL = 8


def draw_inverse(key, part):
    key = jax.random.fold_in(key, 7)
    first, second = jax.random.split(key)
    rows = lax.broadcasted_iota(jnp.int32, (2, NB, NB), 1)
    cols = lax.broadcasted_iota(jnp.int32, (2, NB, NB), 2)
    diag = jax.random.uniform(first, (2, NB, NB), jnp.float32, 0.5, 1.5)
    below = jnp.clip(jax.random.normal(second, (2, NB, NB), jnp.float32), -4.0, 4.0)
    below = below / math.sqrt(NB)
    return jnp.where(rows == cols, diag, jnp.where(rows > cols, below, jnp.float32(0.0)))


def block_levels(own_key, dims, cuts, low, top_value):
    level = 1.0
    for axis_at, blocks in cuts:
        heights = jax.random.uniform(jax.random.fold_in(jax.random.fold_in(own_key, 6), axis_at), (blocks,), jnp.float32, low / len(cuts), top_value / len(cuts))
        level = level * jnp.repeat(jnp.exp(heights), dims[axis_at] // blocks).reshape((-1,) + (1,) * (len(dims) - 1 - axis_at))
    return level


def bell_draw(stream_key, extent, deviation, bound, cuts=(), kind=jnp.bfloat16):
    drawn = deviation * jax.random.normal(stream_key, extent, jnp.float32)
    if cuts:
        drawn = drawn * block_levels(stream_key, extent, cuts, -0.22, 0.18)
    return jnp.clip(drawn, -bound, bound).astype(kind)


def setup_inputs(seed: int = 0) -> dict:
    splits = jax.random.split(jax.random.key(seed), 5)
    partials = bell_draw(splits[0], (N_COL, BR_DEV, N_ROW, NB, RHS), 0.35, 5.0, ((0, 8), (2, 16)), jnp.float32)
    panel = bell_draw(splits[1], (BR_DEV, N_ROW, NB, 2, NB), NB ** -0.5, 0.1875, ((1, 16), (4, 8)), jnp.float32)
    inverse = draw_inverse(jax.random.fold_in(splits[4], 71), 0)
    rhs_blocks = bell_draw(splits[3], (2, NB, RHS), 1.0, 6.0, (), jnp.float32)
    return {"partials": partials, "panel": panel, "inverse": inverse, "rhs_blocks": rhs_blocks}


def reference(partials, panel, inverse, rhs_blocks):
    width = NB // N_COL
    held = partials
    order = jnp.arange(BR_DEV, dtype=jnp.int32)[:, None] * N_ROW + jnp.arange(N_ROW, dtype=jnp.int32)[None, :]
    outcome = []
    for k in range(2):
        summed = jnp.sum(held[:, 0, k], axis=0)
        block = jnp.dot(inverse[k], rhs_blocks[k] - summed, precision=lax.Precision.HIGHEST, preferred_element_type=jnp.float32)
        tiles = panel[:, :, :, k, :].reshape(BR_DEV, N_ROW, NB, N_COL, width)
        pieces = block.reshape(N_COL, width, RHS)
        update = jnp.einsum("lrnci,ciq->clrnq", tiles, pieces, precision=lax.Precision.HIGHEST, preferred_element_type=jnp.float32)
        held = held + jnp.where((order > k)[None, :, :, None, None], update, jnp.float32(0.0))
        outcome.append(block)
    return held, jnp.stack(outcome)
```

```python
import functools

import jax
import jax.numpy as jnp
from jax import lax
from jax.experimental import pallas as pl
from jax.experimental.pallas import tpu as pltpu
from jax.sharding import PartitionSpec as P

F32 = jnp.float32
BF16 = jnp.bfloat16
NY = 4
NZ = 4
NX = 4
W = 128
NB = 1024
VMEM = pl.BlockSpec(memory_space=pltpu.VMEM)
ANY = pl.BlockSpec(memory_space=pl.ANY)


def params(mib=32):
    return pltpu.CompilerParams(vmem_limit_bytes=mib * 2**20)


def in_vmem(x):
    return pltpu.with_memory_space_constraint(x, pltpu.VMEM)


def vm(shape, dtype=F32):
    return pltpu.VMEM(shape, dtype)


def split(x):
    hi = x.astype(BF16)
    return hi, (x - hi.astype(F32)).astype(BF16)


def dot(a, b):
    return jnp.dot(a, b, preferred_element_type=F32)


def dot3(a, b):
    ah, al = split(a)
    bh, bl = split(b)
    n = b.shape[1]
    both = dot(ah, jnp.concatenate([bh, bl], axis=1))
    return both[:, :n] + (both[:, n:] + dot(al, bh))


def position():
    col = lax.axis_index("col")
    return col // 2, col % 2


def pick_kernel(p_ref, send_ref, keep_ref, sem):
    _, h = position()
    one = pltpu.make_async_copy(p_ref.at[0, :, 1 - h], send_ref, sem.at[0])
    two = pltpu.make_async_copy(p_ref.at[0, :, h], keep_ref, sem.at[1])
    one.start()
    two.start()
    one.wait()
    two.wait()


def pick(partials):
    half = vm((NY, W, W))
    return pl.pallas_call(
        pick_kernel,
        out_shape=(half, half),
        in_specs=[ANY],
        out_specs=(VMEM, VMEM),
        scratch_shapes=[pltpu.SemaphoreType.DMA((2,))],
        compiler_params=params(),
        name="pick",
    )(partials.reshape(8, NY, 2, W, W))


def fan_kernel(keep_ref, got_ref, *outs):
    y, _ = position()
    for s in range(NY):
        at = (y + s) % NY
        outs[s][...] = keep_ref[at] + got_ref[at]


def fan(keep, got):
    return pl.pallas_call(
        fan_kernel,
        out_shape=tuple(vm((W, W)) for _ in range(NY)),
        in_specs=[VMEM, VMEM],
        out_specs=(VMEM,) * NY,
        compiler_params=params(),
        name="fan",
    )(in_vmem(keep), in_vmem(got))


def right_kernel(k, rhs_ref, a, b, c, d, out_ref):
    y, h = position()
    at = pl.multiple_of((2 * y + h) * W, W)
    out_ref[...] = rhs_ref[k, pl.ds(at, W), :] - ((a[...] + b[...]) + (c[...] + d[...]))


def right(k, rhs, pieces):
    return pl.pallas_call(
        functools.partial(right_kernel, k),
        out_shape=vm((W, W)),
        in_specs=[VMEM] * 5,
        out_specs=VMEM,
        compiler_params=params(),
        name="right",
    )(in_vmem(rhs), *[in_vmem(p) for p in pieces])


def lay_kernel(a, b, c, d, out_ref):
    y, _ = position()
    for s, piece in enumerate((a, b, c, d)):
        out_ref[(y + NY - s) % NY] = piece[...]


def lay(pieces):
    return pl.pallas_call(
        lay_kernel,
        out_shape=vm((NY, W, W)),
        in_specs=[VMEM] * NY,
        out_specs=VMEM,
        compiler_params=params(),
        name="lay",
    )(*[in_vmem(p) for p in pieces])


def whole(mine_ref, other_ref, all_ref):
    _, h = position()
    for at in range(NY):
        all_ref[at, h] = mine_ref[at]
        all_ref[at, 1 - h] = other_ref[at]
    return all_ref[...].reshape(NB, W)


def first_kernel(inv_ref, mine_ref, other_ref, ph_ref, pl_ref, part_ref, solved_ref, send_ref, keep_ref, all_ref):
    _, h = position()
    block = dot3(inv_ref[0], whole(mine_ref, other_ref, all_ref))
    solved_ref[...] = block
    bh, bl = split(block)
    both = jnp.concatenate([bh, bl], axis=1)
    for at in range(NY):
        for parity, out_ref in ((1 - h, send_ref), (h, keep_ref)):
            rows = pl.ds(pl.multiple_of((2 * at + parity) * W, W), W)
            prod = dot(ph_ref[0, rows, :W], both)
            out_ref[at] = part_ref[0, rows, :] + (
                prod[:, :W] + (prod[:, W:] + dot(pl_ref[0, rows, :W], bh))
            )


def first(inverse, mine, other, p_hi, p_lo, partials):
    half = vm((NY, W, W))
    return pl.pallas_call(
        first_kernel,
        out_shape=(vm((W, W)), half, half),
        in_specs=[VMEM] * 6,
        out_specs=(VMEM,) * 3,
        scratch_shapes=[pltpu.VMEM((NY, 2, W, W), F32)],
        compiler_params=params(),
        name="first",
    )(*[in_vmem(v) for v in (inverse, mine, other, p_hi, p_lo, partials)])


def second_kernel(inv_ref, mine_ref, other_ref, y0_ref, out_ref, all_ref):
    out_ref[0] = y0_ref[...]
    out_ref[1] = dot3(inv_ref[1], whole(mine_ref, other_ref, all_ref))


def second(inverse, mine, other, y0):
    return pl.pallas_call(
        second_kernel,
        out_shape=vm((2, W, W)),
        in_specs=[VMEM] * 4,
        out_specs=VMEM,
        scratch_shapes=[pltpu.VMEM((NY, 2, W, W), F32)],
        compiler_params=params(),
        name="second",
    )(*[in_vmem(v) for v in (inverse, mine, other, y0)])


def parts_kernel(panel_ref, hi_ref, lo_ref):
    rows = hi_ref.shape[1]
    for k in range(2):
        hi, lo = split(panel_ref[0, pl.ds(k, rows, stride=2), :])
        hi_ref[0, :, k * W : (k + 1) * W] = hi
        lo_ref[0, :, k * W : (k + 1) * W] = lo


def parts(panel):
    out = jax.ShapeDtypeStruct((8, NB, 2 * W), BF16)
    spec = pl.BlockSpec((1, NB, 2 * W), lambda i: (i, 0, 0))
    return pl.pallas_call(
        parts_kernel,
        out_shape=(out, out),
        grid=(8,),
        in_specs=[pl.BlockSpec((1, 2 * NB, W), lambda i: (i, 0, 0))],
        out_specs=(spec, spec),
        compiler_params=params(),
        cost_estimate=pl.CostEstimate(flops=10**7, bytes_accessed=16 * 2**20, transcendentals=0),
        name="parts",
    )(panel.reshape(8, 2 * NB, W))


STEP = 256


def update_kernel(y_ref, ph_ref, pl_ref, part_ref, out_ref, solved_ref, buf, both_ref, sem):
    row = lax.axis_index("row")
    x = row // NZ
    block = jnp.where(x == 0, y_ref[0], y_ref[1] + y_ref[2] + y_ref[3])
    solved_ref[...] = block

    def weights(slot, keep0, keep1):
        y0 = jnp.where(keep0, block[0], 0.0)
        y1 = jnp.where(keep1, block[1], 0.0)
        h, l = split(jnp.concatenate([y0, y1], axis=0))
        both_ref[slot] = jnp.concatenate([h, l], axis=1)

    weights(0, row > 0, row > 1)
    weights(1, row >= 0, row >= 0)
    per = NB // STEP

    def copy(i):
        l, j = i // per, i % per
        rows = pl.ds(pl.multiple_of(j * STEP, STEP), STEP)
        return pltpu.make_async_copy(buf.at[l, rows, :], out_ref.at[l, rows, :], sem.at[i])

    def body(i, _):
        l, j = i // per, i % per
        rows = pl.ds(pl.multiple_of(j * STEP, STEP), STEP)
        w = both_ref[jnp.minimum(l, 1)]
        prod = dot(ph_ref[l, rows, :], w)
        low = dot(pl_ref[l, rows, :], w[:, :W])
        buf[l, rows, :] = part_ref[l, rows, :] + (prod[:, :W] + (prod[:, W:] + low))
        copy(i).start()
        return 0

    lax.fori_loop(0, 8 * per, body, 0)

    def done(i, _):
        copy(i).wait()
        return 0

    lax.fori_loop(0, 8 * per, done, 0)


def update(y, p_hi, p_lo, partials):
    return pl.pallas_call(
        update_kernel,
        out_shape=(jax.ShapeDtypeStruct((8, NB, W), F32), jax.ShapeDtypeStruct((2, W, W), F32)),
        in_specs=[VMEM] * 4,
        out_specs=(ANY, VMEM),
        scratch_shapes=[
            pltpu.VMEM((8, NB, W), F32),
            pltpu.VMEM((2, 2 * W, 2 * W), BF16),
            pltpu.SemaphoreType.DMA((8 * NB // STEP,)),
        ],
        compiler_params=params(),
        name="update",
    )(y, *[in_vmem(v) for v in (p_hi, p_lo, partials)])


def swap(x):
    return lax.ppermute(x, "col", [(i, i ^ 1) for i in range(8)])


def along_y(x, s):
    return lax.ppermute(x, "col", [(i, (i + 2 * s) % 8) for i in range(8)])


def to_next_row(x, s):
    pairs = [(c, 8 + (c + 2 * s) % 8) for c in range(8)]
    return lax.ppermute(x, ("row", "col"), pairs)


def gather(pieces):
    mine = lay(pieces)
    return mine, swap(mine)


def per_device(partials, panel, inverse, rhs):
    partials = partials.reshape(8, NB, W)
    send, keep = pick(partials)
    own, *others = fan(keep, swap(send))
    w0 = right(0, rhs, [own] + [along_y(v, s) for s, v in zip((1, 2, 3), others)])
    p_hi, p_lo = parts(panel)
    mine, other = gather([to_next_row(w0, s) for s in range(4)])
    y0, send, keep = first(inverse, mine, other, p_hi, p_lo, partials)
    own, *others = fan(keep, swap(send))
    w1 = right(1, rhs, [own] + [along_y(v, s) for s, v in zip((1, 2, 3), others)])
    mine, other = gather([w1] + [along_y(w1, s) for s in (1, 2, 3)])
    y = second(inverse, mine, other, y0)
    row = lax.axis_index("row")
    got = [lax.ppermute(y, "row", [(1, z)]) for z in (0, 2, 3)]
    y = jnp.where(row == 1, y, got[0] + got[1] + got[2])
    got = [lax.ppermute(y, "row", [(z, z + NZ * s) for z in range(NZ)]) for s in (1, 2, 3)]
    new, solved = update(jnp.stack([y] + got), p_hi, p_lo, partials)
    return new[None, :, None], solved


def solution(mesh):
    return jax.shard_map(
        per_device,
        mesh=mesh,
        in_specs=(
            P("col", None, "row", None, None),
            P(None, "row", None, None, "col"),
            P(None, "col", None),
            P(),
        ),
        out_specs=(P("col", None, "row", None, None), P(None, "col", None)),
        check_vma=False,
    )
```

```python
import functools

import jax
import jax.numpy as jnp
from jax import lax
from jax.experimental import pallas as pl
from jax.experimental.pallas import tpu as pltpu
from jax.sharding import PartitionSpec as P

F32 = jnp.float32
BF16 = jnp.bfloat16
NZ = 4
W = 128
NB = 1024
HALF = NB // 2
VMEM = pl.BlockSpec(memory_space=pltpu.VMEM)
ANY = pl.BlockSpec(memory_space=pl.ANY)


def in_vmem(x):
    return pltpu.with_memory_space_constraint(x, pltpu.VMEM)


def in_hbm(x):
    return pltpu.with_memory_space_constraint(x, pltpu.HBM)


def vm(shape, dtype=F32):
    return pltpu.VMEM(shape, dtype)


def call(kernel, name, out, hbm=(), vmem=(), deps=(), scratch=(), mib=4, out_specs=None):
    return pl.pallas_call(
        kernel,
        out_shape=out,
        in_specs=[ANY] * len(hbm) + [VMEM] * len(vmem) + [ANY] * len(deps),
        out_specs=out_specs or (VMEM,) * len(out),
        scratch_shapes=scratch,
        compiler_params=pltpu.CompilerParams(vmem_limit_bytes=mib * 2**20),
        name=name,
    )(*[in_hbm(v) for v in hbm], *[in_vmem(v) for v in vmem], *deps)


def split(x):
    hi = x.astype(BF16)
    return hi, (x - hi.astype(F32)).astype(BF16)


def dot(a, b):
    return jnp.dot(a, b, preferred_element_type=F32)


def pair_of(b):
    bh, bl = split(b)
    return jnp.concatenate([bh, bl], axis=1)


def dot3(a, both):
    ah, al = split(a)
    prod = dot(ah, both)
    return prod[:, :W] + (prod[:, W:] + dot(al, both[:, :W]))


def core():
    return lax.rem(lax.axis_index("col"), 2)


def half(h):
    return pl.ds(pl.multiple_of(h * HALF, HALF), HALF)


def pick_kernel(p_ref, send_ref, keep_ref, sem):
    h = core()
    one = pltpu.make_async_copy(p_ref.at[0, half(1 - h), :], send_ref, sem.at[0])
    two = pltpu.make_async_copy(p_ref.at[0, half(h), :], keep_ref, sem.at[1])
    one.start()
    two.start()
    one.wait()
    two.wait()


def pick(partials):
    out = vm((HALF, W))
    return call(pick_kernel, "pick", (out, out), hbm=(partials,), scratch=[pltpu.SemaphoreType.DMA((2,))])


def prep_kernel(panel_ref, inv_ref, rhs_ref, dep_ref, ts_ref, tk_ref, is_ref, ik_ref, r_ref, buf, sem):
    h = core()
    copies = []
    for i, (at, inv_out) in enumerate(((1 - h, is_ref), (h, ik_ref))):
        rows = pl.ds(pl.multiple_of(at * NB, NB), NB)
        copies.append(pltpu.make_async_copy(panel_ref.at[0, rows, :], buf.at[i], sem.at[2 * i]))
        copies.append(pltpu.make_async_copy(inv_ref.at[:, :, half(at)], inv_out, sem.at[2 * i + 1]))
    copies.append(pltpu.make_async_copy(rhs_ref.at[:, half(h), :], r_ref, sem.at[4]))
    for c in copies:
        c.start()
    for c in copies:
        c.wait()
    ts_ref[...] = buf[0, pl.ds(0, HALF, stride=2), :]
    tk_ref[...] = buf[1, pl.ds(0, HALF, stride=2), :]


def prep(panel, inverse, rhs, dep):
    return call(
        prep_kernel,
        "prep",
        (vm((HALF, W)), vm((HALF, W)), vm((2, W, HALF)), vm((2, W, HALF)), vm((2, HALF, W))),
        hbm=(panel, inverse, rhs),
        deps=(dep,),
        scratch=[pltpu.VMEM((2, NB, W), F32), pltpu.SemaphoreType.DMA((5,))],
    )


def add_kernel(a_ref, b_ref, out_ref):
    out_ref[...] = a_ref[...] + b_ref[...]


def add(a, b):
    return call(add_kernel, "add", (vm(a.shape),), vmem=(a, b))[0]


def join_kernel(keep_ref, got_ref, out_ref):
    h = core()
    out_ref[h] = keep_ref[...]
    out_ref[1 - h] = got_ref[...]


def join(keep, got):
    return call(join_kernel, "join", (vm((2, HALF, W)),), vmem=(keep, got))[0]


def first_kernel(rhs_ref, a, b, c, d, ik_ref, ig_ref, z_ref, s_ref):
    h = core()
    total = (a[...] + b[...]) + (c[...] + d[...])
    s_ref[...] = total
    both = pair_of(rhs_ref[0] - total)
    z_ref[h] = dot3(ik_ref[0], both)
    z_ref[1 - h] = dot3(ig_ref[0], both)


def first(rhs, sums, ik, ig):
    return call(first_kernel, "first", (vm((2, W, W)), vm((HALF, W))), vmem=(rhs, *sums, ik, ig))


def fold_kernel(z_ref, got_ref, tile_ref, y_ref, u_ref):
    block = z_ref[...] + got_ref[...]
    y_ref[...] = block
    u_ref[...] = dot3(tile_ref[0], pair_of(block[0])) + dot3(tile_ref[1], pair_of(block[1]))


def fold(z, got, tile):
    return call(fold_kernel, "fold", (vm((2, W, W)), vm((HALF, W))), vmem=(z, got, tile))


def second_kernel(rhs_ref, a, b, c, d, s_ref, ik_ref, ig_ref, dep_ref, send_ref, keep_ref):
    total = ((a[...] + b[...]) + (c[...] + d[...])) + s_ref[...]
    both = pair_of(rhs_ref[1] - total)
    keep_ref[...] = dot3(ik_ref[1], both)
    send_ref[...] = dot3(ig_ref[1], both)


def second(rhs, sums, s, ik, ig, dep):
    return call(
        second_kernel, "second", (vm((W, W)), vm((W, W))), vmem=(rhs, *sums, s, ik, ig), deps=(dep,)
    )


def stack_kernel(y_ref, keep_ref, got_ref, out_ref):
    out_ref[0] = y_ref[core()]
    out_ref[1] = keep_ref[...] + got_ref[...]


def stack(y0, keep, got):
    return call(stack_kernel, "stack", (vm((2, W, W)),), vmem=(y0, keep, got))[0]


def choose_kernel(a, b, c, d, out_ref):
    z = lax.rem(lax.axis_index("row"), NZ)
    for m, got in enumerate((a, b, c, d)):

        @pl.when(z == m)
        def _():
            out_ref[...] = got[...]


def choose(got):
    return call(choose_kernel, "choose", (vm((2, W, W)),), vmem=got)[0]


def parts_kernel(panel_ref, p_ref, dep_ref, hi_ref, lo_ref, part_ref, buf, sem):
    bring = pltpu.make_async_copy(p_ref, part_ref, sem.at[8])
    copies = [pltpu.make_async_copy(panel_ref.at[l], buf.at[l], sem.at[l]) for l in range(8)]
    for c in copies:
        c.start()
    bring.start()
    for l in range(8):
        copies[l].wait()
        for k in range(2):
            hi, lo = split(buf[l, pl.ds(k, NB, stride=2), :])
            hi_ref[l, :, k * W : (k + 1) * W] = hi
            lo_ref[l, :, k * W : (k + 1) * W] = lo
    bring.wait()


def parts(panel, partials, dep):
    out = vm((8, NB, 2 * W), BF16)
    return call(
        parts_kernel,
        "parts",
        (out, out, vm((8, NB, W))),
        hbm=(panel, partials),
        deps=(dep,),
        scratch=[pltpu.VMEM((8, 2 * NB, W), F32), pltpu.SemaphoreType.DMA((9,))],
        mib=12,
    )


STEP = 512


def update_kernel(a, b, c, d, ph_ref, pl_ref, part_ref, out_ref, solved_ref, buf, sem):
    row = lax.axis_index("row")
    x = row // NZ
    for m, got in enumerate((a, b, c, d)):

        @pl.when(x == m)
        def _():
            solved_ref[...] = got[...]

    y0 = solved_ref[0]
    y1 = solved_ref[1]
    per = NB // STEP
    head = jnp.concatenate([jnp.where(row > 0, y0, 0.0), jnp.where(row > 1, y1, 0.0)], axis=0)
    rest = jnp.concatenate([y0, y1], axis=0)

    def copy(l, j):
        rows = pl.ds(pl.multiple_of(j * STEP, STEP), STEP)
        return pltpu.make_async_copy(buf.at[l, rows, :], out_ref.at[l, rows, :], sem.at[l * per + j])

    def piece(l, j, w):
        rows = pl.ds(pl.multiple_of(j * STEP, STEP), STEP)
        prod = dot(ph_ref[l, rows, :], w)
        low = dot(pl_ref[l, rows, :], w[:, :W])
        buf[l, rows, :] = part_ref[l, rows, :] + (prod[:, :W] + (prod[:, W:] + low))
        copy(l, j).start()

    w = pair_of(head)
    for j in range(per):
        piece(0, j, w)
    w = pair_of(rest)

    def body(l, _):
        for j in range(per):
            piece(l, j, w)
        return 0

    lax.fori_loop(1, 8, body, 0)

    def done(l, _):
        for j in range(per):
            copy(l, j).wait()
        return 0

    lax.fori_loop(0, 8, done, 0)


def update(got, p_hi, p_lo, partials):
    return call(
        update_kernel,
        "update",
        (jax.ShapeDtypeStruct((8, NB, W), F32), jax.ShapeDtypeStruct((2, W, W), F32)),
        vmem=(*got, p_hi, p_lo, partials),
        out_specs=(ANY, VMEM),
        scratch=[pltpu.VMEM((8, NB, W), F32), pltpu.SemaphoreType.DMA((8 * NB // STEP,))],
        mib=10,
    )


def exchange(x, row_mask, col_mask):
    pairs = [(r * 8 + c, (r ^ row_mask) * 8 + (c ^ col_mask)) for r in range(16) for c in range(8)]
    return lax.ppermute(x, ("row", "col"), pairs)


def swap(x):
    return exchange(x, 0, 1)


def chips(x):
    return [x] + [exchange(x, 0, 2 * m) for m in (2, 1, 3)]


def per_device(partials, panel, inverse, rhs):
    partials = partials.reshape(8, NB, W)
    panel = panel.reshape(8, 2 * NB, W)
    send, keep = pick(partials)
    got = swap(send)
    tile_send, tile_keep, inv_send, inv_keep, rhs = prep(panel, inverse, rhs, send)
    inv_got = swap(inv_send)
    tile = exchange(join(tile_keep, swap(tile_send)), 1, 0)
    z, total = first(rhs, chips(add(keep, got)), inv_keep, inv_got)
    total = exchange(total, 1, 0)
    y0, u = fold(z, swap(z), tile)
    p_hi, p_lo, held = parts(panel, partials, u)
    send, keep = second(rhs, chips(u), total, inv_keep, inv_got, p_hi)
    y = stack(y0, keep, swap(send))
    y = choose([exchange(y, m, 1) for m in range(4)])
    new, solved = update([exchange(y, NZ * m, 1) for m in range(4)], p_hi, p_lo, held)
    return new[None, :, None], solved


def solution(mesh):
    return jax.shard_map(
        per_device,
        mesh=mesh,
        in_specs=(
            P("col", None, "row", None, None),
            P(None, "row", None, None, "col"),
            P(None, "col", None),
            P(),
        ),
        out_specs=(P("col", None, "row", None, None), P(None, "col", None)),
        check_vma=False,
    )
```

```python
import functools

import jax
import jax.numpy as jnp
from jax import lax
from jax.experimental import pallas as pl
from jax.experimental.pallas import tpu as pltpu
from jax.sharding import PartitionSpec as P

F32 = jnp.float32
BF16 = jnp.bfloat16
NZ = 4
W = 128
NB = 1024
PACK = NB // 4
VMEM = pl.BlockSpec(memory_space=pltpu.VMEM)
ANY = pl.BlockSpec(memory_space=pl.ANY)


def in_vmem(x):
    return pltpu.with_memory_space_constraint(x, pltpu.VMEM)


def in_hbm(x):
    return pltpu.with_memory_space_constraint(x, pltpu.HBM)


def vm(shape, dtype=F32):
    return pltpu.VMEM(shape, dtype)


PACKED = vm((PACK, W))


def call(kernel, name, out, hbm=(), vmem=(), deps=(), scratch=(), mib=4, out_specs=None, mb=None, aliases={}):
    return pl.pallas_call(
        kernel,
        out_shape=out,
        in_specs=[ANY] * len(hbm) + [VMEM] * len(vmem) + [ANY] * len(deps),
        out_specs=out_specs or (VMEM,) * len(out),
        scratch_shapes=scratch,
        compiler_params=pltpu.CompilerParams(vmem_limit_bytes=mib * 2**20),
        input_output_aliases=aliases,
        cost_estimate=mb and pl.CostEstimate(flops=0, bytes_accessed=mb * 2**20, transcendentals=0),
        name=name,
    )(*[in_hbm(v) for v in hbm], *[in_vmem(v) for v in vmem], *deps)


def split(x):
    hi = x.astype(BF16)
    return hi, (x - hi.astype(F32)).astype(BF16)


def dot(a, b):
    return jnp.dot(a, b, preferred_element_type=F32)


def pair_of(b):
    bh, bl = split(b)
    return jnp.concatenate([bh, bl], axis=1)


def dot3(a, both):
    ah, al = split(a)
    prod = dot(ah, both)
    return prod[:, :W] + (prod[:, W:] + dot(al, both[:, :W]))


def core():
    return lax.rem(lax.axis_index("col"), 2)


def odd_row():
    return lax.rem(lax.axis_index("row"), 2)


def lane_group(shape):
    return lax.broadcasted_iota(jnp.int32, shape, 1) // 32


def pack(src, b):
    out = None
    for g in range(4):
        rows = src[PACK * g : PACK * (g + 1)]
        shift = 32 * ((g - b) % 4)
        rows = pltpu.roll(rows, shift, 1) if shift else rows
        out = rows if out is None else jnp.where(lane_group(rows.shape) == g, rows, out)
    return out


def unpack(p):
    out = []
    for g in range(4):
        m = jnp.where(lane_group(p.shape) == g, p, 0.0)
        m = m + pltpu.roll(m, 32, 1)
        out.append(m + pltpu.roll(m, 64, 1))
    return jnp.concatenate(out, axis=0)


def start_kernel(p_ref, send_ref, keep_ref, p_buf, q_buf, sem):
    h = core()
    one = pltpu.make_async_copy(p_ref.at[0], p_buf, sem.at[0])
    one.start()
    one.wait()
    for b in range(4):
        q_buf[b] = pack(p_buf, b)
    for r in range(2):
        keep_ref[r] = q_buf[2 * r + h]
        send_ref[r] = q_buf[2 * r + 1 - h]


def start(partials):
    return call(
        start_kernel,
        "start",
        (vm((2, PACK, W)), vm((2, PACK, W))),
        hbm=(partials,),
        scratch=[pltpu.VMEM((NB, W), F32), pltpu.VMEM((4, PACK, W), F32), pltpu.SemaphoreType.DMA((1,))],
    )


def tile_kernel(panel_ref, dep_ref, out_ref, buf, sem):
    copy = pltpu.make_async_copy(panel_ref.at[0], buf, sem.at[0])
    copy.start()
    copy.wait()
    out_ref[...] = buf[pl.ds(0, NB, stride=2), :]


def first_tile(panel, dep):
    return call(
        tile_kernel,
        "tile",
        (vm((NB, W)),),
        hbm=(panel,),
        deps=(dep,),
        scratch=[pltpu.VMEM((2 * NB, W), F32), pltpu.SemaphoreType.DMA((1,))],
        mb=8,
    )[0]


def prep_kernel(inv_ref, rhs_ref, dep_ref, inv_out, rhs_out, r_buf, q_buf, sem):
    one = pltpu.make_async_copy(rhs_ref, r_buf, sem.at[0])
    two = pltpu.make_async_copy(inv_ref, inv_out, sem.at[1])
    one.start()
    two.start()
    one.wait()
    b = 2 * odd_row() + core()
    for k in range(2):
        for at in range(4):
            q_buf[at] = pack(r_buf.at[k], at)
        rhs_out[k] = q_buf[b]
    two.wait()


def prep(inverse, rhs, dep):
    return call(
        prep_kernel,
        "prep",
        (vm((2, W, NB)), vm((2, PACK, W))),
        hbm=(inverse, rhs),
        deps=(dep,),
        scratch=[
            pltpu.VMEM((2, NB, W), F32),
            pltpu.VMEM((4, PACK, W), F32),
            pltpu.SemaphoreType.DMA((2,)),
        ],
        mb=8,
    )


def add_kernel(a_ref, b_ref, mine_ref, other_ref):
    r = odd_row()
    mine_ref[...] = a_ref[r] + b_ref[r]
    other_ref[...] = a_ref[1 - r] + b_ref[1 - r]


def add(a, b):
    return call(add_kernel, "add", (PACKED, PACKED), vmem=(a, b))


def order_kernel(mine_ref, got_ref, _, even_ref, odd_ref, same_ref):
    r = odd_row()

    @pl.when(r == 0)
    def _():
        even_ref[...] = mine_ref[...]
        odd_ref[...] = got_ref[...]

    @pl.when(r == 1)
    def _():
        even_ref[...] = got_ref[...]
        odd_ref[...] = mine_ref[...]


def order(mine, got, tile):
    return call(
        order_kernel, "order", (PACKED, PACKED, vm((NB, W))), vmem=(mine, got, tile), aliases={2: 2}
    )


def odd_kernel(own_ref, got_ref, dep0, dep1, dep2, dep3, out_ref):
    r = odd_row()

    @pl.when(r == 1)
    def _():
        out_ref[...] = own_ref[...]

    @pl.when(r == 0)
    def _():
        out_ref[...] = got_ref[...]


def odd_tile(own, got, deps):
    return call(odd_kernel, "odd", (vm((NB, W)),), vmem=(own, got), deps=deps)[0]


def first_kernel(rhs_ref, a, b, c, d, odd_ref, own_ref, got_ref, t_own, t_got, y_ref, u_ref):
    total = (a[...] + b[...]) + (c[...] + d[...])
    both = pair_of(unpack(rhs_ref[0] - total))
    y_own = dot3(own_ref[0], both)
    y_got = dot3(got_ref[0], both)
    y_ref[0] = y_own
    y_ref[1] = y_got
    own, got = pair_of(y_own), pair_of(y_got)
    out = odd_ref[...]
    group = lane_group(out.shape)
    for g in range(4):
        rows = pl.ds(PACK * g, PACK)
        u = dot3(t_own[rows, :], own) + dot3(t_got[rows, :], got)
        out = jnp.where(group == g, out + u, out)
    u_ref[...] = out


def first(rhs, sums, odd, own, got, t_own, t_got):
    return call(
        first_kernel,
        "first",
        (vm((2, W, W)), PACKED),
        vmem=(rhs, *sums, odd, own, got, t_own, t_got),
        mib=8,
    )


def second_kernel(rhs_ref, a, b, c, d, own_ref, got_ref, y_ref, dep_ref, keep_ref, send_ref):
    total = (a[...] + b[...]) + (c[...] + d[...])
    both = pair_of(unpack(rhs_ref[1] - total))
    group = lane_group((W, W))
    keep_ref[...] = jnp.where(group < 2, y_ref[0], dot3(own_ref[1], both))
    send_ref[...] = jnp.where(group < 2, y_ref[1], dot3(got_ref[1], both))


def second(rhs, sums, own, got, y0, dep):
    return call(
        second_kernel,
        "second",
        (vm((W, W)), vm((W, W))),
        vmem=(rhs, *sums, own, got, y0),
        deps=(dep,),
        mib=8,
    )


def merge_kernel(keep_ref, got_ref, out_ref):
    mine = lane_group((W, W)) % 2 == core()
    out_ref[...] = jnp.where(mine, keep_ref[...], got_ref[...])


def merge(keep, got):
    return call(merge_kernel, "merge", (vm((W, W)),), vmem=(keep, got))[0]


def choose_kernel(a, b, c, d, out_ref):
    x = lax.axis_index("row") // NZ
    for m, got in enumerate((a, b, c, d)):

        @pl.when(x == m)
        def _():
            out_ref[...] = got[...]


def choose(got):
    return call(choose_kernel, "choose", (vm((W, W)),), vmem=got)[0]


GROUP = 4


def parts_kernel(group, panel_ref, p_ref, dep_ref, hi_ref, lo_ref, part_ref, buf, sem):
    bring = pltpu.make_async_copy(p_ref.at[pl.ds(group * GROUP, GROUP)], part_ref, sem.at[GROUP])
    copies = [
        pltpu.make_async_copy(panel_ref.at[group * GROUP + l], buf.at[l], sem.at[l]) for l in range(GROUP)
    ]
    for c in copies:
        c.start()
    bring.start()
    for l in range(GROUP):
        copies[l].wait()
        for k in range(2):
            hi, lo = split(buf[l, pl.ds(k, NB, stride=2), :])
            hi_ref[l, :, k * W : (k + 1) * W] = hi
            lo_ref[l, :, k * W : (k + 1) * W] = lo
    bring.wait()


def parts(group, panel, partials, dep):
    out = vm((GROUP, NB, 2 * W), BF16)
    return call(
        functools.partial(parts_kernel, group),
        "parts",
        (out, out, vm((GROUP, NB, W))),
        hbm=(panel, partials),
        deps=(dep,),
        scratch=[pltpu.VMEM((GROUP, 2 * NB, W), F32), pltpu.SemaphoreType.DMA((GROUP + 1,))],
        mib=6,
        mb=12,
    )


STEP = 512


def update_kernel(a, b, c, d, ph0, pl0, part0, ph1, pl1, part1, out_ref, solved_ref, buf, sides, sem):
    row = lax.axis_index("row")
    z = lax.rem(row, NZ)
    for m, got in enumerate((a, b, c, d)):

        @pl.when(z == m)
        def _():
            sides[0] = got[...]

        @pl.when(z == m ^ 1)
        def _():
            sides[1] = got[...]

    left, right = sides[0], sides[1]
    low_half = lane_group((W, W)) < 2
    y0 = jnp.where(low_half, left, pltpu.roll(right, 64, 1))
    y1 = jnp.where(low_half, pltpu.roll(left, 64, 1), right)
    solved_ref[0] = y0
    solved_ref[1] = y1
    per = NB // STEP
    head = jnp.concatenate([jnp.where(row > 0, y0, 0.0), jnp.where(row > 1, y1, 0.0)], axis=0)
    rest = jnp.concatenate([y0, y1], axis=0)

    def copy(l, j):
        rows = pl.ds(pl.multiple_of(j * STEP, STEP), STEP)
        return pltpu.make_async_copy(buf.at[l, rows, :], out_ref.at[l, rows, :], sem.at[l * per + j])

    def block(group, l, w):
        hi, lo, part = ((ph0, pl0, part0), (ph1, pl1, part1))[group]
        for j in range(per):
            rows = pl.ds(j * STEP, STEP)
            prod = dot(hi[l, rows, :], w)
            low = dot(lo[l, rows, :], w[:, :W])
            at = group * GROUP + l
            buf[at, rows, :] = part[l, rows, :] + (prod[:, :W] + (prod[:, W:] + low))
            copy(at, j).start()

    block(0, 0, pair_of(head))
    w = pair_of(rest)

    def body(group, l, _):
        block(group, l, w)
        return 0

    lax.fori_loop(1, GROUP, functools.partial(body, 0), 0)
    lax.fori_loop(0, GROUP, functools.partial(body, 1), 0)

    def done(l, _):
        for j in range(per):
            copy(l, j).wait()
        return 0

    lax.fori_loop(0, 8, done, 0)


def update(got, parts0, parts1):
    return call(
        update_kernel,
        "update",
        (jax.ShapeDtypeStruct((8, NB, W), F32), jax.ShapeDtypeStruct((2, W, W), F32)),
        vmem=(*got, *parts0, *parts1),
        out_specs=(ANY, VMEM),
        scratch=[
            pltpu.VMEM((8, NB, W), F32),
            pltpu.VMEM((2, W, W), F32),
            pltpu.SemaphoreType.DMA((8 * NB // STEP,)),
        ],
        mib=10,
    )


def exchange(x, row_mask, col_mask):
    pairs = [(r * 8 + c, (r ^ row_mask) * 8 + (c ^ col_mask)) for r in range(16) for c in range(8)]
    return lax.ppermute(x, ("row", "col"), pairs)


def swap(x):
    return exchange(x, 0, 1)


def chips(x):
    return [x] + [exchange(x, 0, 2 * m) for m in (1, 2, 3)]


def rows_over(y, step):
    return [y] + [exchange(y, step * m, 0) for m in (1, 2, 3)]


def per_device(partials, panel, inverse, rhs):
    partials = partials.reshape(8, NB, W)
    panel = panel.reshape(8, 2 * NB, W)
    send, keep = start(partials)
    mine, other = add(keep, swap(send))
    tile = first_tile(panel, send)
    inv, rhs = prep(inverse, rhs, mine)
    inv_got = swap(inv)
    even, odd, tile = order(mine, exchange(other, 1, 0), tile)
    parts0 = parts(0, panel, partials, even)
    sums = chips(even)
    tile = odd_tile(tile, exchange(tile, 1, 0), (*sums[1:], parts0[0]))
    tile_got = swap(tile)
    y0, u = first(rhs, sums, odd, inv, inv_got, tile, tile_got)
    parts1 = parts(1, panel, partials, u)
    keep, send = second(rhs, chips(u), inv, inv_got, y0, parts1[0])
    y = choose(rows_over(merge(keep, swap(send)), NZ))
    new, solved = update(rows_over(y, 1), parts0, parts1)
    return new[None, :, None], solved


def solution(mesh):
    return jax.shard_map(
        per_device,
        mesh=mesh,
        in_specs=(
            P("col", None, "row", None, None),
            P(None, "row", None, None, "col"),
            P(None, "col", None),
            P(),
        ),
        out_specs=(P("col", None, "row", None, None), P(None, "col", None)),
        check_vma=False,
    )
```

```python
import functools

import jax
import jax.numpy as jnp
from jax import lax
from jax.experimental import pallas as pl
from jax.experimental.pallas import tpu as pltpu
from jax.sharding import PartitionSpec as P

F32 = jnp.float32
BF16 = jnp.bfloat16
NZ = 4
W = 128
NB = 1024
PACK = NB // 4
VMEM = pl.BlockSpec(memory_space=pltpu.VMEM)
ANY = pl.BlockSpec(memory_space=pl.ANY)


def in_vmem(x):
    return pltpu.with_memory_space_constraint(x, pltpu.VMEM)


def in_hbm(x):
    return pltpu.with_memory_space_constraint(x, pltpu.HBM)


def vm(shape, dtype=F32):
    return pltpu.VMEM(shape, dtype)


PACKED = vm((PACK, W))


def call(kernel, name, out, hbm=(), vmem=(), deps=(), scratch=(), mib=4, out_specs=None, mb=None, aliases={}):
    return pl.pallas_call(
        kernel,
        out_shape=out,
        in_specs=[ANY] * len(hbm) + [VMEM] * len(vmem) + [ANY] * len(deps),
        out_specs=out_specs or (VMEM,) * len(out),
        scratch_shapes=scratch,
        compiler_params=pltpu.CompilerParams(vmem_limit_bytes=mib * 2**20),
        input_output_aliases=aliases,
        cost_estimate=mb and pl.CostEstimate(flops=0, bytes_accessed=mb * 2**20, transcendentals=0),
        name=name,
    )(*[in_hbm(v) for v in hbm], *[in_vmem(v) for v in vmem], *deps)


def split(x):
    hi = x.astype(BF16)
    return hi, (x - hi.astype(F32)).astype(BF16)


def dot(a, b):
    return jnp.dot(a, b, preferred_element_type=F32)


def pair_of(b):
    bh, bl = split(b)
    return jnp.concatenate([bh, bl], axis=1)


def lhs_of(*blocks):
    parts = [split(b) for b in blocks]
    return jnp.concatenate([hi for hi, _ in parts] + [lo for _, lo in parts], axis=0)


def dot3(lhs, both):
    n = lhs.shape[0] // 2
    prod = dot(lhs, both)
    return prod[:n, :W] + (prod[:n, W:] + prod[n:, :W])


def core():
    return lax.rem(lax.axis_index("col"), 2)


def chip():
    return lax.axis_index("col") // 2


def side():
    return lax.rem(core() + chip() + odd_row(), 2)


def odd_row():
    return lax.rem(lax.axis_index("row"), 2)


def lane_group(shape):
    return lax.broadcasted_iota(jnp.int32, shape, 1) // 32


def on_chain(kernel):
    @functools.wraps(kernel)
    def gated(*refs):
        @pl.when(lax.axis_index("row") < 2)
        def _():
            kernel(*refs)

    return gated


def pack(src, b):
    out = None
    for g in range(4):
        rows = src[PACK * g : PACK * (g + 1)]
        shift = 32 * ((g - b) % 4)
        rows = pltpu.roll(rows, shift, 1) if shift else rows
        out = rows if out is None else jnp.where(lane_group(rows.shape) == g, rows, out)
    return out


def unpack(p):
    out = []
    for g in range(4):
        m = jnp.where(lane_group(p.shape) == g, p, 0.0)
        m = m + pltpu.roll(m, 32, 1)
        out.append(m + pltpu.roll(m, 64, 1))
    return jnp.concatenate(out, axis=0)


@on_chain
def start_kernel(p_ref, panel_ref, send_ref, keep_ref, tile_ref, p_buf, t_buf, q_buf, sem):
    h = side()
    one = pltpu.make_async_copy(p_ref.at[0], p_buf, sem.at[0])
    two = pltpu.make_async_copy(panel_ref.at[0], t_buf, sem.at[1])
    one.start()
    two.start()
    one.wait()
    for b in range(4):
        q_buf[b] = pack(p_buf, b)
    for r in range(2):
        keep_ref[r] = q_buf[2 * r + h]
        send_ref[r] = q_buf[2 * r + 1 - h]
    two.wait()
    tile_ref[...] = t_buf[pl.ds(0, NB, stride=2), :]


def start(partials, panel):
    return call(
        start_kernel,
        "start",
        (vm((2, PACK, W)), vm((2, PACK, W)), vm((NB, W))),
        hbm=(partials, panel),
        scratch=[
            pltpu.VMEM((NB, W), F32),
            pltpu.VMEM((2 * NB, W), F32),
            pltpu.VMEM((4, PACK, W), F32),
            pltpu.SemaphoreType.DMA((2,)),
        ],
    )


@on_chain
def prep_kernel(inv_ref, rhs_ref, dep_ref, inv_out, rhs_out, r_buf, q_buf, sem):
    one = pltpu.make_async_copy(rhs_ref, r_buf, sem.at[0])
    two = pltpu.make_async_copy(inv_ref, inv_out, sem.at[1])
    one.start()
    two.start()
    one.wait()
    b = 2 * odd_row() + side()
    for k in range(2):
        for at in range(4):
            q_buf[at] = pack(r_buf.at[k], at)
        rhs_out[k] = q_buf[b]
    two.wait()


def prep(inverse, rhs, dep):
    return call(
        prep_kernel,
        "prep",
        (vm((2, W, NB)), vm((2, PACK, W))),
        hbm=(inverse, rhs),
        deps=(dep,),
        scratch=[
            pltpu.VMEM((2, NB, W), F32),
            pltpu.VMEM((4, PACK, W), F32),
            pltpu.SemaphoreType.DMA((2,)),
        ],
        mb=8,
    )


@on_chain
def add_kernel(a_ref, b_ref, mine_ref, other_ref):
    r = odd_row()
    mine_ref[...] = a_ref[r] + b_ref[r]
    other_ref[...] = a_ref[1 - r] + b_ref[1 - r]


def add(a, b):
    return call(add_kernel, "add", (PACKED, PACKED), vmem=(a, b))


@on_chain
def order_kernel(mine_ref, got_ref, _, even_ref, odd_ref, same_ref):
    r = odd_row()

    @pl.when(r == 0)
    def _():
        even_ref[...] = mine_ref[...]
        odd_ref[...] = got_ref[...]

    @pl.when(r == 1)
    def _():
        even_ref[...] = got_ref[...]
        odd_ref[...] = mine_ref[...]


def order(mine, got, inv):
    return call(
        order_kernel, "order", (PACKED, PACKED, vm(inv.shape)), vmem=(mine, got, inv), aliases={2: 2}
    )


@on_chain
def odd_kernel(own_ref, got_ref, dep0, dep1, dep2, dep3, out_ref):
    r = odd_row()

    @pl.when(r == 1)
    def _():
        out_ref[...] = own_ref[...]

    @pl.when(r == 0)
    def _():
        out_ref[...] = got_ref[...]


def odd_tile(own, got, deps):
    return call(odd_kernel, "odd", (vm((NB, W)),), vmem=(own, got), deps=deps)[0]


@on_chain
def first_kernel(rhs_ref, a, b, c, d, odd_ref, own_ref, got_ref, t_a, t_b, y_ref, u_ref):
    total = (a[...] + b[...]) + (c[...] + d[...])
    y = dot3(lhs_of(own_ref[0], got_ref[0]), pair_of(unpack(rhs_ref[0] - total)))
    y_ref[0] = y[:W]
    y_ref[1] = y[W:]
    both = pair_of(jnp.where(odd_row() == 1, y, jnp.concatenate([y[W:], y[:W]], axis=0)))
    out = odd_ref[...]
    group = lane_group(out.shape)
    for g in range(4):
        rows = pl.ds(PACK * g, PACK)
        hi, lo = split(jnp.concatenate([t_a[rows, :], t_b[rows, :]], axis=1))
        prod = dot(hi, both)
        u = prod[:, :W] + (prod[:, W:] + dot(lo, both[:, :W]))
        out = jnp.where(group == g, out + u, out)
    u_ref[...] = out


def first(rhs, sums, odd, own, got, t_a, t_b):
    return call(
        first_kernel,
        "first",
        (vm((2, W, W)), PACKED),
        vmem=(rhs, *sums, odd, own, got, t_a, t_b),
        mib=8,
    )


@on_chain
def second_kernel(rhs_ref, a, b, c, d, own_ref, got_ref, y_ref, dep_ref, out_ref):
    total = (a[...] + b[...]) + (c[...] + d[...])
    y = dot3(lhs_of(own_ref[1], got_ref[1]), pair_of(unpack(rhs_ref[1] - total)))
    group = lane_group((W, W))
    own = jnp.where(group < 2, y_ref[0], y[:W])
    got = jnp.where(group < 2, y_ref[1], y[W:])
    out_ref[...] = jnp.where(group % 2 == core(), own, got)


def second(rhs, sums, own, got, y0, dep):
    return call(
        second_kernel, "second", (vm((W, W)),), vmem=(rhs, *sums, own, got, y0), deps=(dep,), mib=8
    )[0]


def choose_kernel(a, b, c, d, out_ref):
    x = lax.axis_index("row") // NZ
    for m, got in enumerate((a, b, c, d)):

        @pl.when(x == m)
        def _():
            out_ref[...] = got[...]


def choose(got):
    return call(choose_kernel, "choose", (vm((W, W)),), vmem=got)[0]


GROUP = 4


def parts_kernel(group, panel_ref, p_ref, dep_ref, hi_ref, lo_ref, part_ref, buf, sem):
    bring = pltpu.make_async_copy(p_ref.at[pl.ds(group * GROUP, GROUP)], part_ref, sem.at[GROUP])
    copies = [
        pltpu.make_async_copy(panel_ref.at[group * GROUP + l], buf.at[l], sem.at[l]) for l in range(GROUP)
    ]
    for c in copies:
        c.start()
    bring.start()
    for l in range(GROUP):
        copies[l].wait()
        for k in range(2):
            hi, lo = split(buf[l, pl.ds(k, NB, stride=2), :])
            hi_ref[l, :, k * W : (k + 1) * W] = hi
            lo_ref[l, :, k * W : (k + 1) * W] = lo
    bring.wait()


def parts(group, panel, partials, dep):
    out = vm((GROUP, NB, 2 * W), BF16)
    return call(
        functools.partial(parts_kernel, group),
        "parts",
        (out, out, vm((GROUP, NB, W))),
        hbm=(panel, partials),
        deps=(dep,),
        scratch=[pltpu.VMEM((GROUP, 2 * NB, W), F32), pltpu.SemaphoreType.DMA((GROUP + 1,))],
        mib=6,
        mb=12,
    )


def deal_kernel(a, b, c, d, keep_ref, send_ref, sides):
    z = lax.rem(lax.axis_index("row"), NZ)
    for m, got in enumerate((a, b, c, d)):

        @pl.when(z == m)
        def _():
            sides[0] = got[...]

        @pl.when(z == m ^ 1)
        def _():
            sides[1] = got[...]

    left, right = sides[0], sides[1]
    group = lane_group((W, W))

    def lanes(parts):
        (p, i), (q, j), (r, k), (t, n) = parts
        turn = lambda v, shift: pltpu.roll(v, shift, 1) if shift else v
        low = jnp.where(group == 0, turn(p, i), turn(q, j))
        return jnp.where(group < 2, low, jnp.where(group == 2, turn(r, k), turn(t, n)))

    zero = lanes(((left, 0), (left, 96), (right, 64), (right, 32)))
    one = lanes(((left, 96), (left, 64), (right, 32), (right, 0)))
    h = core()
    keep_ref[...] = jnp.where(h == 0, zero, one)
    send_ref[...] = jnp.where(h == 0, one, zero)


def deal(got):
    return call(
        deal_kernel, "deal", (vm((W, W)), vm((W, W))), vmem=got, scratch=[pltpu.VMEM((2, W, W), F32)]
    )


def update_kernel(keep_ref, got_ref, ph0, pl0, part0, ph1, pl1, part1, out_ref, solved_ref, buf, sem):
    row = lax.axis_index("row")
    x, z = row // NZ, lax.rem(row, NZ)
    way = core() + chip() + jnp.where(x == 0, 0, 1)
    left = lax.rem(way + jnp.where(z == 0, 0, 1), 2)
    right = lax.rem(way + jnp.where(z == 1, 0, 1) + 1, 2)
    group = lane_group((W, W))
    mine = group == jnp.where(group < 2, left, 2 + right)
    keep, got = keep_ref[...], got_ref[...]
    even = group % 2 == 0

    def block(k):
        if k == 0:
            spread = lambda v: jnp.where(even, v, pltpu.roll(v, 32, 1))
        else:
            spread = lambda v: jnp.where(even, pltpu.roll(v, 96, 1), v)
        return jnp.where(mine, spread(keep), spread(got))

    y0, y1 = block(0), block(1)
    solved_ref[0] = y0
    solved_ref[1] = y1
    head = pair_of(jnp.concatenate([jnp.where(row > 0, y0, 0.0), jnp.where(row > 1, y1, 0.0)], axis=0))
    rest = pair_of(jnp.concatenate([y0, y1], axis=0))

    def copy(l):
        return pltpu.make_async_copy(buf.at[l], out_ref.at[l], sem.at[l])

    for l in range(8):
        hi, lo, part = ((ph0, pl0, part0), (ph1, pl1, part1))[l // GROUP]
        w = head if l == 0 else rest
        prod = dot(hi[l % GROUP], w)
        low = dot(lo[l % GROUP], w[:, :W])
        buf[l] = part[l % GROUP] + (prod[:, :W] + (prod[:, W:] + low))
        copy(l).start()
    for l in range(8):
        copy(l).wait()


def update(keep, got, parts0, parts1):
    return call(
        update_kernel,
        "update",
        (jax.ShapeDtypeStruct((8, NB, W), F32), jax.ShapeDtypeStruct((2, W, W), F32)),
        vmem=(keep, got, *parts0, *parts1),
        out_specs=(ANY, VMEM),
        scratch=[
            pltpu.VMEM((8, NB, W), F32),
            pltpu.SemaphoreType.DMA((8,)),
        ],
        mib=10,
    )


def exchange(x, row_mask, col_mask):
    pairs = [(r * 8 + c, (r ^ row_mask) * 8 + (c ^ col_mask)) for r in range(16) for c in range(8)]
    return lax.ppermute(x, ("row", "col"), pairs)


def swap(x):
    return exchange(x, 0, 1)


def chips(x):
    return [x] + [exchange(x, 0, mask) for mask in (3, 4, 7)]


def rows_over(y, step):
    return [y] + [exchange(y, step * m, 1) for m in (1, 2, 3)]


def per_device(partials, panel, inverse, rhs):
    partials = partials.reshape(8, NB, W)
    panel = panel.reshape(8, 2 * NB, W)
    send, keep, tile = start(partials, panel)
    tile_odd = exchange(tile, 1, 1)
    mine, other = add(keep, swap(send))
    inv, rhs = prep(inverse, rhs, mine)
    even, odd, inv = order(mine, exchange(other, 1, 1), inv)
    inv_got = swap(inv)
    parts0 = parts(0, panel, partials, even)
    sums = chips(even)
    tile = odd_tile(tile, tile_odd, (*sums[1:], parts0[0]))
    y0, u = first(rhs, sums, odd, inv, inv_got, tile, swap(tile))
    parts1 = parts(1, panel, partials, u)
    y = second(rhs, chips(u), inv, inv_got, y0, parts1[0])
    keep, send = deal(rows_over(choose(rows_over(y, NZ)), 1))
    new, solved = update(keep, swap(send), parts0, parts1)
    return new[None, :, None], solved


def solution(mesh):
    return jax.shard_map(
        per_device,
        mesh=mesh,
        in_specs=(
            P("col", None, "row", None, None),
            P(None, "row", None, None, "col"),
            P(None, "col", None),
            P(),
        ),
        out_specs=(P("col", None, "row", None, None), P(None, "col", None)),
        check_vma=False,
    )
```

```python
import functools

import jax
import jax.numpy as jnp
from jax import lax
from jax.experimental import pallas as pl
from jax.experimental.pallas import tpu as pltpu
from jax.sharding import PartitionSpec as P

F32 = jnp.float32
BF16 = jnp.bfloat16
NZ = 4
X_STEPS = (0, 2, 3, 1)
Z_STEPS = (0, 1, 3, 2)
W = 128
NB = 1024
PACK = NB // 4
VMEM = pl.BlockSpec(memory_space=pltpu.VMEM)
ANY = pl.BlockSpec(memory_space=pl.ANY)


def in_vmem(x):
    return pltpu.with_memory_space_constraint(x, pltpu.VMEM)


def in_hbm(x):
    return pltpu.with_memory_space_constraint(x, pltpu.HBM)


def vm(shape, dtype=F32):
    return pltpu.VMEM(shape, dtype)


PACKED = vm((PACK, W))


def call(kernel, name, out, hbm=(), vmem=(), deps=(), scratch=(), mib=4, out_specs=None, mb=None, aliases={}):
    return pl.pallas_call(
        kernel,
        out_shape=out,
        in_specs=[ANY] * len(hbm) + [VMEM] * len(vmem) + [ANY] * len(deps),
        out_specs=out_specs or (VMEM,) * len(out),
        scratch_shapes=scratch,
        compiler_params=pltpu.CompilerParams(vmem_limit_bytes=mib * 2**20),
        input_output_aliases=aliases,
        cost_estimate=mb and pl.CostEstimate(flops=0, bytes_accessed=mb * 2**20, transcendentals=0),
        name=name,
    )(*[in_hbm(v) for v in hbm], *[in_vmem(v) for v in vmem], *deps)


def split(x):
    hi = x.astype(BF16)
    return hi, (x - hi.astype(F32)).astype(BF16)


def dot(a, b):
    return jnp.dot(a, b, preferred_element_type=F32)


def pair_of(b):
    bh, bl = split(b)
    return jnp.concatenate([bh, bl], axis=1)


def lhs_of(*blocks):
    parts = [split(b) for b in blocks]
    return jnp.concatenate([hi for hi, _ in parts] + [lo for _, lo in parts], axis=0)


def dot3(lhs, both):
    n = lhs.shape[0] // 2
    prod = dot(lhs, both)
    return prod[:n, :W] + (prod[:n, W:] + prod[n:, :W])


def core():
    return lax.rem(lax.axis_index("col"), 2)


def chip():
    return lax.axis_index("col") // 2


def side():
    return lax.rem(core() + chip() + odd_row(), 2)


def odd_row():
    return lax.rem(lax.axis_index("row"), 2)


def lane_group(shape):
    return lax.broadcasted_iota(jnp.int32, shape, 1) // 32


def on_chain(kernel):
    @functools.wraps(kernel)
    def gated(*refs):
        @pl.when(lax.axis_index("row") < 2)
        def _():
            kernel(*refs)

    return gated


def pack(src, b):
    out = None
    for g in range(4):
        rows = src[PACK * g : PACK * (g + 1)]
        shift = 32 * ((g - b) % 4)
        rows = pltpu.roll(rows, shift, 1) if shift else rows
        out = rows if out is None else jnp.where(lane_group(rows.shape) == g, rows, out)
    return out


def unpack(p):
    out = []
    for g in range(4):
        m = jnp.where(lane_group(p.shape) == g, p, 0.0)
        m = m + pltpu.roll(m, 32, 1)
        out.append(m + pltpu.roll(m, 64, 1))
    return jnp.concatenate(out, axis=0)


@on_chain
def start_kernel(p_ref, panel_ref, send_ref, keep_ref, tile_ref, p_buf, t_buf, q_buf, sem):
    h = side()
    one = pltpu.make_async_copy(p_ref.at[0], p_buf, sem.at[0])
    two = pltpu.make_async_copy(panel_ref.at[0], t_buf, sem.at[1])
    one.start()
    two.start()
    one.wait()
    for b in range(4):
        q_buf[b] = pack(p_buf, b)
    for r in range(2):
        keep_ref[r] = q_buf[2 * r + h]
        send_ref[r] = q_buf[2 * r + 1 - h]
    two.wait()
    tile_ref[...] = t_buf[pl.ds(0, NB, stride=2), :]


def start(partials, panel):
    return call(
        start_kernel,
        "start",
        (vm((2, PACK, W)), vm((2, PACK, W)), vm((NB, W))),
        hbm=(partials, panel),
        scratch=[
            pltpu.VMEM((NB, W), F32),
            pltpu.VMEM((2 * NB, W), F32),
            pltpu.VMEM((4, PACK, W), F32),
            pltpu.SemaphoreType.DMA((2,)),
        ],
    )


@on_chain
def prep_kernel(inv_ref, rhs_ref, dep_ref, inv_out, rhs_out, r_buf, q_buf, sem):
    one = pltpu.make_async_copy(rhs_ref, r_buf, sem.at[0])
    two = pltpu.make_async_copy(inv_ref, inv_out, sem.at[1])
    one.start()
    two.start()
    one.wait()
    b = 2 * odd_row() + side()
    for k in range(2):
        for at in range(4):
            q_buf[at] = pack(r_buf.at[k], at)
        rhs_out[k] = q_buf[b]
    two.wait()


def prep(inverse, rhs, dep):
    return call(
        prep_kernel,
        "prep",
        (vm((2, W, NB)), vm((2, PACK, W))),
        hbm=(inverse, rhs),
        deps=(dep,),
        scratch=[
            pltpu.VMEM((2, NB, W), F32),
            pltpu.VMEM((4, PACK, W), F32),
            pltpu.SemaphoreType.DMA((2,)),
        ],
        mb=8,
    )


@on_chain
def add_kernel(a_ref, b_ref, mine_ref, other_ref):
    r = odd_row()
    mine_ref[...] = a_ref[r] + b_ref[r]
    other_ref[...] = a_ref[1 - r] + b_ref[1 - r]


def add(a, b):
    return call(add_kernel, "add", (PACKED, PACKED), vmem=(a, b))


@on_chain
def order_kernel(mine_ref, got_ref, _, even_ref, odd_ref, same_ref):
    r = odd_row()

    @pl.when(r == 0)
    def _():
        even_ref[...] = mine_ref[...]
        odd_ref[...] = got_ref[...]

    @pl.when(r == 1)
    def _():
        even_ref[...] = got_ref[...]
        odd_ref[...] = mine_ref[...]


def order(mine, got, inv):
    return call(
        order_kernel, "order", (PACKED, PACKED, vm(inv.shape)), vmem=(mine, got, inv), aliases={2: 2}
    )


@on_chain
def odd_kernel(own_ref, got_ref, dep0, dep1, dep2, dep3, out_ref):
    r = odd_row()

    @pl.when(r == 1)
    def _():
        out_ref[...] = own_ref[...]

    @pl.when(r == 0)
    def _():
        out_ref[...] = got_ref[...]


def odd_tile(own, got, deps):
    return call(odd_kernel, "odd", (vm((NB, W)),), vmem=(own, got), deps=deps)[0]


@on_chain
def rows_kernel(own_ref, got_ref, out_ref):
    for k in range(2):
        out_ref[k] = lhs_of(own_ref[k], got_ref[k])


def inverse_rows(own, got):
    return call(rows_kernel, "rows", (vm((2, 4 * W, NB), BF16),), vmem=(own, got), mib=8)[0]


def times_tile(out, tile_ref, y):
    both = pair_of(y)
    group = lane_group(out.shape)
    for g in range(4):
        u = dot3(lhs_of(tile_ref[pl.ds(PACK * g, PACK), :]), both)
        out = jnp.where(group == g, out + u, out)
    return out


@on_chain
def first_kernel(rhs_ref, a, b, c, d, inv_ref, y_ref):
    total = (a[...] + b[...]) + (c[...] + d[...])
    y = dot3(inv_ref[0], pair_of(unpack(rhs_ref[0] - total)))
    y_ref[0] = y[:W]
    y_ref[1] = y[W:]


def first(rhs, sums, inv):
    return call(first_kernel, "first", (vm((2, W, W)),), vmem=(rhs, *sums, inv), mib=8)[0]


@on_chain
def rest_kernel(turn, u_ref, y_ref, tile_ref, out_ref):
    y = jnp.where(odd_row() == turn, y_ref[0], y_ref[1])
    out_ref[...] = times_tile(u_ref[...], tile_ref, y)


def rest(turn, u, y, tile):
    return call(functools.partial(rest_kernel, turn), "rest", (PACKED,), vmem=(u, y, tile), mib=8)[0]


@on_chain
def second_kernel(rhs_ref, a, b, c, d, inv_ref, y_ref, dep_ref, out_ref):
    total = (a[...] + b[...]) + (c[...] + d[...])
    y = dot3(inv_ref[1], pair_of(unpack(rhs_ref[1] - total)))
    group = lane_group((W, W))
    own = jnp.where(group < 2, y_ref[0], y[:W])
    got = jnp.where(group < 2, y_ref[1], y[W:])
    out_ref[...] = jnp.where(group % 2 == core(), own, got)


def second(rhs, sums, inv, y0, dep):
    return call(
        second_kernel, "second", (vm((W, W)),), vmem=(rhs, *sums, inv, y0), deps=(dep,), mib=8
    )[0]


def choose_kernel(a, b, c, d, out_ref):
    x = lax.axis_index("row") // NZ
    for m, got in zip(X_STEPS, (a, b, c, d)):

        @pl.when(x == m)
        def _():
            out_ref[...] = got[...]


def choose(got):
    return call(choose_kernel, "choose", (vm((W, W)),), vmem=got)[0]


GROUP = 4


def parts_kernel(group, panel_ref, p_ref, dep_ref, hi_ref, lo_ref, part_ref, buf, sem):
    bring = pltpu.make_async_copy(p_ref.at[pl.ds(group * GROUP, GROUP)], part_ref, sem.at[GROUP])
    copies = [
        pltpu.make_async_copy(panel_ref.at[group * GROUP + l], buf.at[l], sem.at[l]) for l in range(GROUP)
    ]
    for c in copies:
        c.start()
    bring.start()
    for l in range(GROUP):
        copies[l].wait()
        for k in range(2):
            hi, lo = split(buf[l, pl.ds(k, NB, stride=2), :])
            hi_ref[l, :, k * W : (k + 1) * W] = hi
            lo_ref[l, :, k * W : (k + 1) * W] = lo
    bring.wait()


def parts(group, panel, partials, dep):
    out = vm((GROUP, NB, 2 * W), BF16)
    return call(
        functools.partial(parts_kernel, group),
        "parts",
        (out, out, vm((GROUP, NB, W))),
        hbm=(panel, partials),
        deps=(dep,),
        scratch=[pltpu.VMEM((GROUP, 2 * NB, W), F32), pltpu.SemaphoreType.DMA((GROUP + 1,))],
        mib=6,
        mb=12,
    )


def deal_kernel(a, b, c, d, keep_ref, send_ref, sides):
    z = lax.rem(lax.axis_index("row"), NZ)
    for m, got in zip(Z_STEPS, (a, b, c, d)):

        @pl.when(z == m)
        def _():
            sides[0] = got[...]

        @pl.when(z == m ^ 1)
        def _():
            sides[1] = got[...]

    left, right = sides[0], sides[1]
    group = lane_group((W, W))

    def lanes(parts):
        (p, i), (q, j), (r, k), (t, n) = parts
        turn = lambda v, shift: pltpu.roll(v, shift, 1) if shift else v
        low = jnp.where(group == 0, turn(p, i), turn(q, j))
        return jnp.where(group < 2, low, jnp.where(group == 2, turn(r, k), turn(t, n)))

    zero = lanes(((left, 0), (left, 96), (right, 64), (right, 32)))
    one = lanes(((left, 96), (left, 64), (right, 32), (right, 0)))
    h = core()
    keep_ref[...] = jnp.where(h == 0, zero, one)
    send_ref[...] = jnp.where(h == 0, one, zero)


def deal(got):
    return call(
        deal_kernel, "deal", (vm((W, W)), vm((W, W))), vmem=got, scratch=[pltpu.VMEM((2, W, W), F32)]
    )


def update_kernel(keep_ref, got_ref, ph0, pl0, part0, ph1, pl1, part1, out_ref, solved_ref, buf, sem):
    row = lax.axis_index("row")
    x, z = row // NZ, lax.rem(row, NZ)
    way = core() + chip() + jnp.where(x == 0, 0, 1)
    left = lax.rem(way + jnp.where(z == 0, 0, 1), 2)
    right = lax.rem(way + jnp.where(z == 1, 0, 1) + 1, 2)
    group = lane_group((W, W))
    mine = group == jnp.where(group < 2, left, 2 + right)
    keep, got = keep_ref[...], got_ref[...]
    even = group % 2 == 0

    def block(k):
        if k == 0:
            spread = lambda v: jnp.where(even, v, pltpu.roll(v, 32, 1))
        else:
            spread = lambda v: jnp.where(even, pltpu.roll(v, 96, 1), v)
        return jnp.where(mine, spread(keep), spread(got))

    y0, y1 = block(0), block(1)
    solved_ref[0] = y0
    solved_ref[1] = y1
    head = pair_of(jnp.concatenate([jnp.where(row > 0, y0, 0.0), jnp.where(row > 1, y1, 0.0)], axis=0))
    rest = pair_of(jnp.concatenate([y0, y1], axis=0))

    def copy(l):
        return pltpu.make_async_copy(buf.at[l], out_ref.at[l], sem.at[l])

    for l in range(8):
        hi, lo, part = ((ph0, pl0, part0), (ph1, pl1, part1))[l // GROUP]
        w = head if l == 0 else rest
        prod = dot(hi[l % GROUP], w)
        low = dot(lo[l % GROUP], w[:, :W])
        buf[l] = part[l % GROUP] + (prod[:, :W] + (prod[:, W:] + low))
        copy(l).start()
    for l in range(8):
        copy(l).wait()


def update(keep, got, parts0, parts1):
    return call(
        update_kernel,
        "update",
        (jax.ShapeDtypeStruct((8, NB, W), F32), jax.ShapeDtypeStruct((2, W, W), F32)),
        vmem=(keep, got, *parts0, *parts1),
        out_specs=(ANY, VMEM),
        scratch=[
            pltpu.VMEM((8, NB, W), F32),
            pltpu.SemaphoreType.DMA((8,)),
        ],
        mib=10,
    )


def exchange(x, row_mask, col_mask):
    pairs = [(r * 8 + c, (r ^ row_mask) * 8 + (c ^ col_mask)) for r in range(16) for c in range(8)]
    return lax.ppermute(x, ("row", "col"), pairs)


def swap(x):
    return exchange(x, 0, 1)


def chips(x):
    return [x] + [exchange(x, 0, mask) for mask in (7, 3, 4)]


def step(x, place):
    pairs = [(r * 8 + c, place(r // NZ, r % NZ) * 8 + (c ^ 1)) for r in range(16) for c in range(8)]
    return lax.ppermute(x, ("row", "col"), pairs)


def along_x(y):
    place = lambda m: lambda x, z: (x ^ m) * NZ + z
    return [y] + [step(y, place(m)) for m in X_STEPS[1:]]


def along_z(y):
    place = lambda m: lambda x, z: x * NZ + (z ^ m)
    return [y] + [step(y, place(m)) for m in Z_STEPS[1:]]


def per_device(partials, panel, inverse, rhs):
    partials = partials.reshape(8, NB, W)
    panel = panel.reshape(8, 2 * NB, W)
    send, keep, tile = start(partials, panel)
    tile_odd = exchange(tile, 1, 1)
    mine, other = add(keep, swap(send))
    inv, rhs = prep(inverse, rhs, mine)
    even, odd, inv = order(mine, exchange(other, 1, 1), inv)
    parts0 = parts(0, panel, partials, even)
    inv = inverse_rows(inv, swap(inv))
    sums = chips(even)
    tile = odd_tile(tile, tile_odd, (*sums[1:], parts0[0]))
    y0 = first(rhs, sums, inv)
    u = rest(0, rest(1, odd, y0, tile), y0, swap(tile))
    parts1 = parts(1, panel, partials, u)
    y = second(rhs, chips(u), inv, y0, parts1[0])
    keep, send = deal(along_z(choose(along_x(y))))
    new, solved = update(keep, swap(send), parts0, parts1)
    return new[None, :, None], solved


def solution(mesh):
    return jax.shard_map(
        per_device,
        mesh=mesh,
        in_specs=(
            P("col", None, "row", None, None),
            P(None, "row", None, None, "col"),
            P(None, "col", None),
            P(),
        ),
        out_specs=(P("col", None, "row", None, None), P(None, "col", None)),
        check_vma=False,
    )
```

```python
import functools

import jax
import jax.numpy as jnp
from jax import lax
from jax.experimental import pallas as pl
from jax.experimental.pallas import tpu as pltpu
from jax.sharding import PartitionSpec as P

F32 = jnp.float32
BF16 = jnp.bfloat16
NZ = 4
X_STEPS = (0, 2, 3, 1)
W = 128
NB = 1024
PACK = NB // 4
VMEM = pl.BlockSpec(memory_space=pltpu.VMEM)
ANY = pl.BlockSpec(memory_space=pl.ANY)


def in_vmem(x):
    return pltpu.with_memory_space_constraint(x, pltpu.VMEM)


def in_hbm(x):
    return pltpu.with_memory_space_constraint(x, pltpu.HBM)


def vm(shape, dtype=F32):
    return pltpu.VMEM(shape, dtype)


PACKED = vm((PACK, W))


def call(kernel, name, out, hbm=(), vmem=(), deps=(), scratch=(), mib=4, out_specs=None, mb=None, aliases={}):
    return pl.pallas_call(
        kernel,
        out_shape=out,
        in_specs=[ANY] * len(hbm) + [VMEM] * len(vmem) + [ANY] * len(deps),
        out_specs=out_specs or (VMEM,) * len(out),
        scratch_shapes=scratch,
        compiler_params=pltpu.CompilerParams(vmem_limit_bytes=mib * 2**20),
        input_output_aliases=aliases,
        cost_estimate=mb and pl.CostEstimate(flops=0, bytes_accessed=mb * 2**20, transcendentals=0),
        name=name,
    )(*[in_hbm(v) for v in hbm], *[in_vmem(v) for v in vmem], *deps)


def split(x):
    hi = x.astype(BF16)
    return hi, (x - hi.astype(F32)).astype(BF16)


def dot(a, b):
    return jnp.dot(a, b, preferred_element_type=F32)


def pair_of(b):
    bh, bl = split(b)
    return jnp.concatenate([bh, bl], axis=1)


def lhs_of(*blocks):
    parts = [split(b) for b in blocks]
    return jnp.concatenate([hi for hi, _ in parts] + [lo for _, lo in parts], axis=0)


def dot3(lhs, both):
    n = lhs.shape[0] // 2
    prod = dot(lhs, both)
    return prod[:n, :W] + (prod[:n, W:] + prod[n:, :W])


def core():
    return lax.rem(lax.axis_index("col"), 2)


def chip():
    return lax.axis_index("col") // 2


def side():
    return lax.rem(core() + chip() + odd_row(), 2)


def odd_row():
    return lax.rem(lax.axis_index("row"), 2)


def lane_group(shape):
    return lax.broadcasted_iota(jnp.int32, shape, 1) // 32


def on_chain(kernel):
    @functools.wraps(kernel)
    def gated(*refs):
        @pl.when(lax.axis_index("row") < 2)
        def _():
            kernel(*refs)

    return gated


def packed(rows):
    group = lane_group(rows[0].shape)
    high, odd = group >= 2, group % 2 == 1
    out = list(rows)
    for g in range(2):
        a, b = out[g], out[g + 2]
        turned = pltpu.roll(jnp.where(high, a, b), 64, 1)
        out[g], out[g + 2] = jnp.where(high, turned, a), jnp.where(high, b, turned)
    for g in (0, 2):
        a, b = out[g], out[g + 1]
        out[g], out[g + 1] = jnp.where(odd, pltpu.roll(b, 32, 1), a), jnp.where(odd, b, pltpu.roll(a, 96, 1))
    return out


def unpack(p):
    group = lane_group(p.shape)
    turned = [p] + [pltpu.roll(p, 32 * n, 1) for n in (1, 2, 3)]
    out = []
    for g in range(4):
        m = p
        for n in (1, 2, 3):
            m = jnp.where(group == (g + n) % 4, turned[n], m)
        out.append(m)
    return jnp.concatenate(out, axis=0)


@on_chain
def start_kernel(p_ref, send_ref, keep_ref, p_buf, q_buf, sem):
    h = side()
    copies = [
        pltpu.make_async_copy(p_ref.at[0, pl.ds(PACK * g, PACK), :], p_buf.at[g], sem.at[g]) for g in range(4)
    ]
    for c in copies:
        c.start()
    for c in copies:
        c.wait()
    for b, block in enumerate(packed([p_buf[g] for g in range(4)])):
        q_buf[b] = block
    for r in range(2):
        keep_ref[r] = q_buf[2 * r + h]
        send_ref[r] = q_buf[2 * r + 1 - h]


def start(partials):
    return call(
        start_kernel,
        "start",
        (vm((2, PACK, W)), vm((2, PACK, W))),
        hbm=(partials,),
        scratch=[
            pltpu.VMEM((4, PACK, W), F32),
            pltpu.VMEM((4, PACK, W), F32),
            pltpu.SemaphoreType.DMA((4,)),
        ],
    )


@on_chain
def tile_kernel(panel_ref, dep_ref, out_ref, buf, sem):
    copy = pltpu.make_async_copy(panel_ref.at[0], buf, sem.at[0])
    copy.start()
    copy.wait()
    out_ref[...] = buf[pl.ds(0, NB, stride=2), :]


def first_tile(panel, dep):
    return call(
        tile_kernel,
        "tile",
        (vm((NB, W)),),
        hbm=(panel,),
        deps=(dep,),
        scratch=[pltpu.VMEM((2 * NB, W), F32), pltpu.SemaphoreType.DMA((1,))],
        mb=8,
    )[0]


@on_chain
def prep_kernel(inv_ref, rhs_ref, dep_ref, inv_out, rhs_out, r_buf, q_buf, sem):
    one = pltpu.make_async_copy(rhs_ref, r_buf, sem.at[0])
    two = pltpu.make_async_copy(inv_ref, inv_out, sem.at[1])
    one.start()
    two.start()
    one.wait()
    b = 2 * odd_row() + side()
    for k in range(2):
        for at, block in enumerate(packed([r_buf[k, PACK * g : PACK * (g + 1)] for g in range(4)])):
            q_buf[at] = block
        rhs_out[k] = q_buf[b]
    two.wait()


def prep(inverse, rhs, dep):
    return call(
        prep_kernel,
        "prep",
        (vm((2, W, NB)), vm((2, PACK, W))),
        hbm=(inverse, rhs),
        deps=(dep,),
        scratch=[
            pltpu.VMEM((2, NB, W), F32),
            pltpu.VMEM((4, PACK, W), F32),
            pltpu.SemaphoreType.DMA((2,)),
        ],
        mb=8,
    )


@on_chain
def add_kernel(a_ref, b_ref, dep_ref, mine_ref, other_ref):
    r = odd_row()
    mine_ref[...] = a_ref[r] + b_ref[r]
    other_ref[...] = a_ref[1 - r] + b_ref[1 - r]


def add(a, b, dep):
    return call(add_kernel, "add", (PACKED, PACKED), vmem=(a, b), deps=(dep,))


@on_chain
def order_kernel(mine_ref, got_ref, _, even_ref, odd_ref, same_ref):
    r = odd_row()

    @pl.when(r == 0)
    def _():
        even_ref[...] = mine_ref[...]
        odd_ref[...] = got_ref[...]

    @pl.when(r == 1)
    def _():
        even_ref[...] = got_ref[...]
        odd_ref[...] = mine_ref[...]


def order(mine, got, inv):
    return call(
        order_kernel, "order", (PACKED, PACKED, vm(inv.shape)), vmem=(mine, got, inv), aliases={2: 2}
    )


@on_chain
def odd_kernel(own_ref, got_ref, dep0, dep1, dep2, dep3, out_ref):
    r = odd_row()

    @pl.when(r == 1)
    def _():
        out_ref[...] = own_ref[...]

    @pl.when(r == 0)
    def _():
        out_ref[...] = got_ref[...]


def odd_tile(own, got, deps):
    return call(odd_kernel, "odd", (vm((NB, W)),), vmem=(own, got), deps=deps)[0]


@on_chain
def rows_kernel(own_ref, got_ref, out_ref):
    for k in range(2):
        out_ref[k] = lhs_of(own_ref[k], got_ref[k])


def inverse_rows(own, got):
    return call(rows_kernel, "rows", (vm((2, 4 * W, NB), BF16),), vmem=(own, got), mib=8)[0]


def times_tile(out, tile_ref, y):
    both = pair_of(y)
    group = lane_group(out.shape)
    for g in range(4):
        u = dot3(lhs_of(tile_ref[pl.ds(PACK * g, PACK), :]), both)
        out = jnp.where(group == g, out + u, out)
    return out


@on_chain
def first_kernel(rhs_ref, a, b, c, d, inv_ref, y_ref):
    total = (a[...] + b[...]) + (c[...] + d[...])
    y = dot3(inv_ref[0], pair_of(unpack(rhs_ref[0] - total)))
    y_ref[0] = y[:W]
    y_ref[1] = y[W:]


def first(rhs, sums, inv):
    return call(first_kernel, "first", (vm((2, W, W)),), vmem=(rhs, *sums, inv), mib=8)[0]


@on_chain
def rest_kernel(turn, u_ref, y_ref, tile_ref, out_ref):
    y = jnp.where(odd_row() == turn, y_ref[0], y_ref[1])
    out_ref[...] = times_tile(u_ref[...], tile_ref, y)


def rest(turn, u, y, tile):
    return call(functools.partial(rest_kernel, turn), "rest", (PACKED,), vmem=(u, y, tile), mib=8)[0]


@on_chain
def second_kernel(rhs_ref, a, b, c, d, inv_ref, y_ref, dep_ref, out_ref):
    total = (a[...] + b[...]) + (c[...] + d[...])
    y = dot3(inv_ref[1], pair_of(unpack(rhs_ref[1] - total)))
    group = lane_group((W, W))
    own = jnp.where(group < 2, y_ref[0], y[:W])
    got = jnp.where(group < 2, y_ref[1], y[W:])
    out_ref[...] = jnp.where(group % 2 == core(), own, got)


def second(rhs, sums, inv, y0, dep):
    return call(
        second_kernel, "second", (vm((W, W)),), vmem=(rhs, *sums, inv, y0), deps=(dep,), mib=8
    )[0]


def choose_kernel(a, b, c, d, out_ref):
    x = lax.axis_index("row") // NZ
    for m, got in zip(X_STEPS, (a, b, c, d)):

        @pl.when(x == m)
        def _():
            out_ref[...] = got[...]


def choose(got):
    return call(choose_kernel, "choose", (vm((W, W)),), vmem=got)[0]


GROUP = 4


def parts_kernel(group, panel_ref, p_ref, dep_ref, hi_ref, lo_ref, part_ref, buf, sem):
    bring = pltpu.make_async_copy(p_ref.at[pl.ds(group * GROUP, GROUP)], part_ref, sem.at[GROUP])
    copies = [
        pltpu.make_async_copy(panel_ref.at[group * GROUP + l], buf.at[l], sem.at[l]) for l in range(GROUP)
    ]
    for c in copies:
        c.start()
    bring.start()
    for l in range(GROUP):
        copies[l].wait()
        for k in range(2):
            hi, lo = split(buf[l, pl.ds(k, NB, stride=2), :])
            hi_ref[l, :, k * W : (k + 1) * W] = hi
            lo_ref[l, :, k * W : (k + 1) * W] = lo
    bring.wait()


def parts(group, panel, partials, dep):
    out = vm((GROUP, NB, 2 * W), BF16)
    return call(
        functools.partial(parts_kernel, group),
        "parts",
        (out, out, vm((GROUP, NB, W))),
        hbm=(panel, partials),
        deps=(dep,),
        scratch=[pltpu.VMEM((GROUP, 2 * NB, W), F32), pltpu.SemaphoreType.DMA((GROUP + 1,))],
        mib=6,
        mb=12,
    )


def deal_kernel(a, b, c, d, keep_ref, send_ref, sides):
    z = lax.rem(lax.axis_index("row"), NZ)
    for at, (from_0, from_1) in enumerate(((a, d), (b, a), (d, c), (c, b))):

        @pl.when(z == at)
        def _():
            sides[0] = from_0[...]
            sides[1] = from_1[...]

    left, right = sides[0], sides[1]
    group = lane_group((W, W))

    def lanes(parts):
        (p, i), (q, j), (r, k), (t, n) = parts
        turn = lambda v, shift: pltpu.roll(v, shift, 1) if shift else v
        low = jnp.where(group == 0, turn(p, i), turn(q, j))
        return jnp.where(group < 2, low, jnp.where(group == 2, turn(r, k), turn(t, n)))

    zero = lanes(((left, 0), (left, 96), (right, 64), (right, 32)))
    one = lanes(((left, 96), (left, 64), (right, 32), (right, 0)))
    h = core()
    keep_ref[...] = jnp.where(h == 0, zero, one)
    send_ref[...] = jnp.where(h == 0, one, zero)


def deal(got):
    return call(
        deal_kernel, "deal", (vm((W, W)), vm((W, W))), vmem=got, scratch=[pltpu.VMEM((2, W, W), F32)]
    )


def update_kernel(keep_ref, got_ref, ph0, pl0, part0, ph1, pl1, part1, out_ref, solved_ref, buf, y_buf, sem):
    row = lax.axis_index("row")
    x, z = row // NZ, lax.rem(row, NZ)
    way = core() + chip() + jnp.where(x == 0, 0, 1)
    left = lax.rem(way + jnp.where(z == 0, 0, 1), 2)
    right = lax.rem(way + jnp.where(z == 1, 0, 1) + 1, 2)
    group = lane_group((W, W))
    mine = group == jnp.where(group < 2, left, 2 + right)
    keep, got = keep_ref[...], got_ref[...]
    even = group % 2 == 0

    def block(k):
        if k == 0:
            spread = lambda v: jnp.where(even, v, pltpu.roll(v, 32, 1))
        else:
            spread = lambda v: jnp.where(even, pltpu.roll(v, 96, 1), v)
        return jnp.where(mine, spread(keep), spread(got))

    y0, y1 = block(0), block(1)
    y_buf[0] = y0
    y_buf[1] = y1
    solved = pltpu.make_async_copy(y_buf, solved_ref, sem.at[9])
    solved.start()
    head = pair_of(jnp.concatenate([jnp.where(row > 0, y0, 0.0), jnp.where(row > 1, y1, 0.0)], axis=0))
    rest = pair_of(jnp.concatenate([y0, y1], axis=0))

    pieces = [(l, 0, NB) for l in range(7)] + [(7, 0, NB // 2), (7, NB // 2, NB // 2)]
    copies = []
    for n, (l, at, size) in enumerate(pieces):
        hi, lo, part = ((ph0, pl0, part0), (ph1, pl1, part1))[l // GROUP]
        w = head if l == 0 else rest
        rows = pl.ds(at, size)
        prod = dot(hi[l % GROUP, rows, :], w)
        low = dot(lo[l % GROUP, rows, :], w[:, :W])
        buf[l, rows, :] = part[l % GROUP, rows, :] + (prod[:, :W] + (prod[:, W:] + low))
        copies.append(pltpu.make_async_copy(buf.at[l, rows, :], out_ref.at[l, rows, :], sem.at[n]))
        copies[-1].start()
    for c in copies:
        c.wait()
    solved.wait()


def update(keep, got, parts0, parts1):
    return call(
        update_kernel,
        "update",
        (jax.ShapeDtypeStruct((8, NB, W), F32), jax.ShapeDtypeStruct((2, W, W), F32)),
        vmem=(keep, got, *parts0, *parts1),
        out_specs=(ANY, ANY),
        scratch=[
            pltpu.VMEM((8, NB, W), F32),
            pltpu.VMEM((2, W, W), F32),
            pltpu.SemaphoreType.DMA((10,)),
        ],
        mib=10,
    )


def exchange(x, row_mask, col_mask):
    pairs = []
    for r in range(16):
        for c in range(8):
            chain = r < 2
            pairs.append((r * 8 + c, (r ^ row_mask) * 8 + (c ^ col_mask) if chain else r * 8 + (c ^ 1)))
    return lax.ppermute(x, ("row", "col"), pairs)


def swap(x):
    return exchange(x, 0, 1)


def chips(x):
    return [x] + [exchange(x, 0, mask) for mask in (7, 3, 4)]


def step(x, place):
    pairs = [(r * 8 + c, place(r // NZ, r % NZ) * 8 + (c ^ 1)) for r in range(16) for c in range(8)]
    return lax.ppermute(x, ("row", "col"), pairs)


def along_x(y):
    cycles = {1: {0: 1, 1: 0}, 2: {0: 2, 2: 1, 1: 0}, 3: {0: 3, 3: 0}}
    place = lambda m: lambda x, z: (cycles[m].get(x, x) if z < 2 else x) * NZ + z
    return [y] + [step(y, place(m)) for m in X_STEPS[1:]]


def along_z(y):
    cycles = ({0: 2, 1: 0, 2: 1}, {0: 3, 3: 0, 1: 2, 2: 1}, {0: 1, 1: 3, 3: 0})
    place = lambda cycle: lambda x, z: x * NZ + cycle.get(z, z)
    return [y] + [step(y, place(cycle)) for cycle in cycles[::-1]]


def per_device(partials, panel, inverse, rhs):
    partials = partials.reshape(8, NB, W)
    panel = panel.reshape(8, 2 * NB, W)
    send, keep = start(partials)
    tile = first_tile(panel, send)
    tile_odd = exchange(tile, 1, 1)
    mine, other = add(keep, swap(send), tile)
    inv, rhs = prep(inverse, rhs, mine)
    even, odd, inv = order(mine, exchange(other, 1, 1), inv)
    parts0 = parts(0, panel, partials, even)
    inv = inverse_rows(inv, swap(inv))
    sums = chips(even)
    tile = odd_tile(tile, tile_odd, (*sums[1:], parts0[0]))
    y0 = first(rhs, sums, inv)
    u = rest(0, rest(1, odd, y0, tile), y0, swap(tile))
    parts1 = parts(1, panel, partials, u)
    y = second(rhs, chips(u), inv, y0, parts1[0])
    keep, send = deal(along_z(choose(along_x(y))))
    new, solved = update(keep, swap(send), parts0, parts1)
    return new[None, :, None], solved


def solution(mesh):
    return jax.shard_map(
        per_device,
        mesh=mesh,
        in_specs=(
            P("col", None, "row", None, None),
            P(None, "row", None, None, "col"),
            P(None, "col", None),
            P(),
        ),
        out_specs=(P("col", None, "row", None, None), P(None, "col", None)),
        check_vma=False,
    )
```

```python
import functools

import jax
import jax.numpy as jnp
from jax import lax
from jax.experimental import pallas as pl
from jax.experimental.pallas import tpu as pltpu
from jax.sharding import PartitionSpec as P

F32 = jnp.float32
BF16 = jnp.bfloat16
NZ = 4
X_STEPS = (0, 1, 2, 3)
W = 128
NB = 1024
PACK = NB // 4
VMEM = pl.BlockSpec(memory_space=pltpu.VMEM)
ANY = pl.BlockSpec(memory_space=pl.ANY)


def in_vmem(x):
    return pltpu.with_memory_space_constraint(x, pltpu.VMEM)


def in_hbm(x):
    return pltpu.with_memory_space_constraint(x, pltpu.HBM)


def vm(shape, dtype=F32):
    return pltpu.VMEM(shape, dtype)


PACKED = vm((PACK, W))


def call(kernel, name, out, hbm=(), vmem=(), deps=(), scratch=(), mib=4, out_specs=None, mb=None, aliases={}):
    return pl.pallas_call(
        kernel,
        out_shape=out,
        in_specs=[ANY] * len(hbm) + [VMEM] * len(vmem) + [ANY] * len(deps),
        out_specs=out_specs or (VMEM,) * len(out),
        scratch_shapes=scratch,
        compiler_params=pltpu.CompilerParams(vmem_limit_bytes=mib * 2**20),
        input_output_aliases=aliases,
        cost_estimate=mb and pl.CostEstimate(flops=0, bytes_accessed=mb * 2**20, transcendentals=0),
        name=name,
    )(*[in_hbm(v) for v in hbm], *[in_vmem(v) for v in vmem], *deps)


def split(x):
    hi = x.astype(BF16)
    return hi, (x - hi.astype(F32)).astype(BF16)


def dot(a, b):
    return jnp.dot(a, b, preferred_element_type=F32)


def pair_of(b):
    bh, bl = split(b)
    return jnp.concatenate([bh, bl], axis=1)


def lhs_of(*blocks):
    parts = [split(b) for b in blocks]
    return jnp.concatenate([hi for hi, _ in parts] + [lo for _, lo in parts], axis=0)


def dot3(lhs, both):
    n = lhs.shape[0] // 2
    prod = dot(lhs, both)
    return prod[:n, :W] + (prod[:n, W:] + prod[n:, :W])


def core():
    return lax.rem(lax.axis_index("col"), 2)


def chip():
    return lax.axis_index("col") // 2


def side():
    return lax.rem(core() + chip() + odd_row(), 2)


def odd_row():
    return lax.rem(lax.axis_index("row"), 2)


def lane_group(shape):
    return lax.broadcasted_iota(jnp.int32, shape, 1) // 32


def on_chain(kernel):
    @functools.wraps(kernel)
    def gated(*refs):
        @pl.when(lax.axis_index("row") < 2)
        def _():
            kernel(*refs)

    return gated


def packed(rows):
    group = lane_group(rows[0].shape)
    high, odd = group >= 2, group % 2 == 1
    out = list(rows)
    for g in range(2):
        a, b = out[g], out[g + 2]
        turned = pltpu.roll(jnp.where(high, a, b), 64, 1)
        out[g], out[g + 2] = jnp.where(high, turned, a), jnp.where(high, b, turned)
    for g in (0, 2):
        a, b = out[g], out[g + 1]
        out[g], out[g + 1] = jnp.where(odd, pltpu.roll(b, 32, 1), a), jnp.where(odd, b, pltpu.roll(a, 96, 1))
    return out


def unpack(p):
    group = lane_group(p.shape)
    turned = [p] + [pltpu.roll(p, 32 * n, 1) for n in (1, 2, 3)]
    out = []
    for g in range(4):
        m = p
        for n in (1, 2, 3):
            m = jnp.where(group == (g + n) % 4, turned[n], m)
        out.append(m)
    return jnp.concatenate(out, axis=0)


@on_chain
def start_kernel(p_ref, send_ref, keep_ref, p_buf, q_buf, sem):
    h = side()
    copies = [
        pltpu.make_async_copy(p_ref.at[0, pl.ds(PACK * g, PACK), :], p_buf.at[g], sem.at[g]) for g in range(4)
    ]
    for c in copies:
        c.start()
    for c in copies:
        c.wait()
    for b, block in enumerate(packed([p_buf[g] for g in range(4)])):
        q_buf[b] = block
    for r in range(2):
        keep_ref[r] = q_buf[2 * r + h]
        send_ref[r] = q_buf[2 * r + 1 - h]


def start(partials):
    return call(
        start_kernel,
        "start",
        (vm((2, PACK, W)), vm((2, PACK, W))),
        hbm=(partials,),
        scratch=[
            pltpu.VMEM((4, PACK, W), F32),
            pltpu.VMEM((4, PACK, W), F32),
            pltpu.SemaphoreType.DMA((4,)),
        ],
    )


@on_chain
def tile_kernel(panel_ref, dep_ref, out_ref, buf, sem):
    copy = pltpu.make_async_copy(panel_ref.at[0], buf, sem.at[0])
    copy.start()
    copy.wait()
    out_ref[...] = buf[pl.ds(0, NB, stride=2), :]


def first_tile(panel, dep):
    return call(
        tile_kernel,
        "tile",
        (vm((NB, W)),),
        hbm=(panel,),
        deps=(dep,),
        scratch=[pltpu.VMEM((2 * NB, W), F32), pltpu.SemaphoreType.DMA((1,))],
        mb=8,
    )[0]


@on_chain
def prep_kernel(inv_ref, rhs_ref, dep_ref, inv_out, rhs_out, r_buf, q_buf, sem):
    one = pltpu.make_async_copy(rhs_ref, r_buf, sem.at[0])
    two = pltpu.make_async_copy(inv_ref, inv_out, sem.at[1])
    one.start()
    two.start()
    one.wait()
    b = 2 * odd_row() + side()
    for k in range(2):
        for at, block in enumerate(packed([r_buf[k, PACK * g : PACK * (g + 1)] for g in range(4)])):
            q_buf[at] = block
        rhs_out[k] = q_buf[b]
    two.wait()


def prep(inverse, rhs, dep):
    return call(
        prep_kernel,
        "prep",
        (vm((2, W, NB)), vm((2, PACK, W))),
        hbm=(inverse, rhs),
        deps=(dep,),
        scratch=[
            pltpu.VMEM((2, NB, W), F32),
            pltpu.VMEM((4, PACK, W), F32),
            pltpu.SemaphoreType.DMA((2,)),
        ],
        mb=8,
    )


@on_chain
def add_kernel(a_ref, b_ref, dep_ref, mine_ref, other_ref):
    r = odd_row()
    mine_ref[...] = a_ref[r] + b_ref[r]
    other_ref[...] = a_ref[1 - r] + b_ref[1 - r]


def add(a, b, dep):
    return call(add_kernel, "add", (PACKED, PACKED), vmem=(a, b), deps=(dep,))


@on_chain
def order_kernel(mine_ref, got_ref, _, even_ref, odd_ref, same_ref):
    r = odd_row()

    @pl.when(r == 0)
    def _():
        even_ref[...] = mine_ref[...]
        odd_ref[...] = got_ref[...]

    @pl.when(r == 1)
    def _():
        even_ref[...] = got_ref[...]
        odd_ref[...] = mine_ref[...]


def order(mine, got, inv):
    return call(
        order_kernel, "order", (PACKED, PACKED, vm(inv.shape)), vmem=(mine, got, inv), aliases={2: 2}
    )


@on_chain
def odd_kernel(own_ref, got_ref, dep0, dep1, dep2, dep3, out_ref):
    r = odd_row()

    @pl.when(r == 1)
    def _():
        out_ref[...] = own_ref[...]

    @pl.when(r == 0)
    def _():
        out_ref[...] = got_ref[...]


def odd_tile(own, got, deps):
    return call(odd_kernel, "odd", (vm((NB, W)),), vmem=(own, got), deps=deps)[0]


@on_chain
def rows_kernel(own_ref, got_ref, out_ref):
    for k in range(2):
        out_ref[k] = lhs_of(own_ref[k], got_ref[k])


def inverse_rows(own, got):
    return call(rows_kernel, "rows", (vm((2, 4 * W, NB), BF16),), vmem=(own, got), mib=8)[0]


def times_tile(out, tile_ref, y):
    both = pair_of(y)
    group = lane_group(out.shape)
    for g in range(4):
        u = dot3(lhs_of(tile_ref[pl.ds(PACK * g, PACK), :]), both)
        out = jnp.where(group == g, out + u, out)
    return out


@on_chain
def first_kernel(rhs_ref, a, b, c, d, inv_ref, y_ref):
    total = (a[...] + b[...]) + (c[...] + d[...])
    y = dot3(inv_ref[0], pair_of(unpack(rhs_ref[0] - total)))
    y_ref[0] = y[:W]
    y_ref[1] = y[W:]


def first(rhs, sums, inv):
    return call(first_kernel, "first", (vm((2, W, W)),), vmem=(rhs, *sums, inv), mib=8)[0]


@on_chain
def rest_kernel(turn, u_ref, y_ref, tile_ref, out_ref):
    y = jnp.where(odd_row() == turn, y_ref[0], y_ref[1])
    out_ref[...] = times_tile(u_ref[...], tile_ref, y)


def rest(turn, u, y, tile):
    return call(functools.partial(rest_kernel, turn), "rest", (PACKED,), vmem=(u, y, tile), mib=8)[0]


@on_chain
def second_kernel(rhs_ref, a, b, c, d, inv_ref, y_ref, dep_ref, out_ref):
    total = (a[...] + b[...]) + (c[...] + d[...])
    y = dot3(inv_ref[1], pair_of(unpack(rhs_ref[1] - total)))
    group = lane_group((W, W))
    own = jnp.where(group < 2, y_ref[0], y[:W])
    got = jnp.where(group < 2, y_ref[1], y[W:])
    out_ref[...] = jnp.where(group % 2 == core(), own, got)


def second(rhs, sums, inv, y0, dep):
    return call(
        second_kernel, "second", (vm((W, W)),), vmem=(rhs, *sums, inv, y0), deps=(dep,), mib=8
    )[0]


def choose_kernel(a, b, c, d, out_ref):
    x = lax.axis_index("row") // NZ
    for m, got in zip(X_STEPS, (a, b, c, d)):

        @pl.when(x == m)
        def _():
            out_ref[...] = got[...]


def choose(got):
    return call(choose_kernel, "choose", (vm((W, W)),), vmem=got)[0]


GROUP = 4


def parts_kernel(group, panel_ref, p_ref, dep_ref, hi_ref, lo_ref, part_ref, buf, sem):
    bring = pltpu.make_async_copy(p_ref.at[pl.ds(group * GROUP, GROUP)], part_ref, sem.at[GROUP])
    copies = [
        pltpu.make_async_copy(panel_ref.at[group * GROUP + l], buf.at[l, pl.ds(0, 2 * NB), :], sem.at[l])
        for l in range(GROUP)
    ]
    for c in copies:
        c.start()
    bring.start()
    for l in range(GROUP):
        copies[l].wait()
        for k in range(2):
            hi, lo = split(buf[l, pl.ds(k, NB, stride=2), :])
            hi_ref[l, :, k * W : (k + 1) * W] = hi
            lo_ref[l, :, k * W : (k + 1) * W] = lo
    bring.wait()


def parts(group, panel, partials, dep):
    out = vm((GROUP, NB, 2 * W), BF16)
    return call(
        functools.partial(parts_kernel, group),
        "parts",
        (out, out, vm((GROUP, NB, W))),
        hbm=(panel, partials),
        deps=(dep,),
        scratch=[pltpu.VMEM((GROUP, 2 * NB + 8, W), F32), pltpu.SemaphoreType.DMA((GROUP + 1,))],
        mib=6,
        mb=12,
    )


def deal_kernel(a, b, c, d, keep_ref, send_ref, sides):
    z = lax.rem(lax.axis_index("row"), NZ)
    for at, (from_0, from_1) in enumerate(((a, d), (b, a), (d, c), (c, b))):

        @pl.when(z == at)
        def _():
            sides[0] = from_0[...]
            sides[1] = from_1[...]

    left, right = sides[0], sides[1]
    group = lane_group((W, W))

    def lanes(parts):
        (p, i), (q, j), (r, k), (t, n) = parts
        turn = lambda v, shift: pltpu.roll(v, shift, 1) if shift else v
        low = jnp.where(group == 0, turn(p, i), turn(q, j))
        return jnp.where(group < 2, low, jnp.where(group == 2, turn(r, k), turn(t, n)))

    zero = lanes(((left, 0), (left, 96), (right, 64), (right, 32)))
    one = lanes(((left, 96), (left, 64), (right, 32), (right, 0)))
    h = core()
    keep_ref[...] = jnp.where(h == 0, zero, one)
    send_ref[...] = jnp.where(h == 0, one, zero)


def deal(got):
    return call(
        deal_kernel, "deal", (vm((W, W)), vm((W, W))), vmem=got, scratch=[pltpu.VMEM((2, W, W), F32)]
    )


def update_kernel(keep_ref, got_ref, ph0, pl0, part0, ph1, pl1, part1, out_ref, solved_ref, buf, y_buf, sem):
    row = lax.axis_index("row")
    x, z = row // NZ, lax.rem(row, NZ)
    way = core() + chip() + jnp.where(x == 0, 0, 1)
    left = lax.rem(way + jnp.where(z == 0, 0, 1), 2)
    right = lax.rem(way + jnp.where(z == 1, 0, 1) + 1, 2)
    group = lane_group((W, W))
    mine = group == jnp.where(group < 2, left, 2 + right)
    keep, got = keep_ref[...], got_ref[...]
    even = group % 2 == 0

    def block(k):
        if k == 0:
            spread = lambda v: jnp.where(even, v, pltpu.roll(v, 32, 1))
        else:
            spread = lambda v: jnp.where(even, pltpu.roll(v, 96, 1), v)
        return jnp.where(mine, spread(keep), spread(got))

    y0, y1 = block(0), block(1)
    y_buf[0] = y0
    y_buf[1] = y1
    solved = pltpu.make_async_copy(y_buf, solved_ref, sem.at[9])
    solved.start()
    head = pair_of(jnp.concatenate([jnp.where(row > 0, y0, 0.0), jnp.where(row > 1, y1, 0.0)], axis=0))
    rest = pair_of(jnp.concatenate([y0, y1], axis=0))

    pieces = [(l, 0, NB) for l in range(7)] + [(7, 0, NB // 2), (7, NB // 2, NB // 2)]
    copies = []
    for n, (l, at, size) in enumerate(pieces):
        hi, lo, part = ((ph0, pl0, part0), (ph1, pl1, part1))[l // GROUP]
        w = head if l == 0 else rest
        rows = pl.ds(at, size)
        prod = dot(hi[l % GROUP, rows, :], w)
        low = dot(lo[l % GROUP, rows, :], w[:, :W])
        buf[l, rows, :] = part[l % GROUP, rows, :] + (prod[:, :W] + (prod[:, W:] + low))
        copies.append(pltpu.make_async_copy(buf.at[l, rows, :], out_ref.at[l, rows, :], sem.at[n]))
        copies[-1].start()
    for c in copies:
        c.wait()
    solved.wait()


def update(keep, got, parts0, parts1):
    return call(
        update_kernel,
        "update",
        (jax.ShapeDtypeStruct((8, NB, W), F32), jax.ShapeDtypeStruct((2, W, W), F32)),
        vmem=(keep, got, *parts0, *parts1),
        out_specs=(ANY, ANY),
        scratch=[
            pltpu.VMEM((8, NB, W), F32),
            pltpu.VMEM((2, W, W), F32),
            pltpu.SemaphoreType.DMA((10,)),
        ],
        mib=10,
    )


def exchange(x, row_mask, col_mask):
    pairs = []
    for r in range(16):
        for c in range(8):
            chain = r < 2
            pairs.append((r * 8 + c, (r ^ row_mask) * 8 + (c ^ col_mask) if chain else r * 8 + (c ^ 1)))
    return lax.ppermute(x, ("row", "col"), pairs)


def swap(x):
    return exchange(x, 0, 1)


def chips(x):
    return [x] + [exchange(x, 0, mask) for mask in (7, 3, 4)]


def step(x, place):
    pairs = [(r * 8 + c, place(r // NZ, r % NZ) * 8 + (c ^ 1)) for r in range(16) for c in range(8)]
    return lax.ppermute(x, ("row", "col"), pairs)


def along_x(y):
    cycles = {1: {0: 1, 1: 0}, 2: {0: 2, 2: 1, 1: 0}, 3: {0: 3, 3: 0}}
    place = lambda m: lambda x, z: (cycles[m].get(x, x) if z < 2 else x) * NZ + z
    return [y] + [step(y, place(m)) for m in X_STEPS[1:]]


def along_z(y):
    cycles = ({0: 2, 1: 0, 2: 1}, {0: 3, 3: 0, 1: 2, 2: 1}, {0: 1, 1: 3, 3: 0})
    place = lambda cycle: lambda x, z: x * NZ + cycle.get(z, z)
    return [y] + [step(y, place(cycle)) for cycle in cycles[::-1]]


def per_device(partials, panel, inverse, rhs):
    partials = partials.reshape(8, NB, W)
    panel = panel.reshape(8, 2 * NB, W)
    send, keep = start(partials)
    tile = first_tile(panel, send)
    tile_odd = exchange(tile, 1, 1)
    mine, other = add(keep, swap(send), tile)
    inv, rhs = prep(inverse, rhs, mine)
    even, odd, inv = order(mine, exchange(other, 1, 1), inv)
    parts0 = parts(0, panel, partials, even)
    inv = inverse_rows(inv, swap(inv))
    sums = chips(even)
    tile = odd_tile(tile, tile_odd, (*sums[1:], parts0[0]))
    y0 = first(rhs, sums, inv)
    u = rest(0, rest(1, odd, y0, tile), y0, swap(tile))
    parts1 = parts(1, panel, partials, u)
    y = second(rhs, chips(u), inv, y0, parts1[0])
    keep, send = deal(along_z(choose(along_x(y))))
    new, solved = update(keep, swap(send), parts0, parts1)
    return new[None, :, None], solved


def solution(mesh):
    return jax.shard_map(
        per_device,
        mesh=mesh,
        in_specs=(
            P("col", None, "row", None, None),
            P(None, "row", None, None, "col"),
            P(None, "col", None),
            P(),
        ),
        out_specs=(P("col", None, "row", None, None), P(None, "col", None)),
        check_vma=False,
    )
```

```python
import functools

import jax
import jax.numpy as jnp
from jax import lax
from jax.experimental import pallas as pl
from jax.experimental.pallas import tpu as pltpu
from jax.sharding import PartitionSpec as P

F32 = jnp.float32
BF16 = jnp.bfloat16
NZ = 4
X_STEPS = (0, 1, 2, 3)
W = 128
NB = 1024
PACK = NB // 4
VMEM = pl.BlockSpec(memory_space=pltpu.VMEM)
ANY = pl.BlockSpec(memory_space=pl.ANY)


def in_vmem(x):
    return pltpu.with_memory_space_constraint(x, pltpu.VMEM)


def in_hbm(x):
    return pltpu.with_memory_space_constraint(x, pltpu.HBM)


def vm(shape, dtype=F32):
    return pltpu.VMEM(shape, dtype)


PACKED = vm((PACK, W))


def call(kernel, name, out, hbm=(), vmem=(), deps=(), scratch=(), mib=4, out_specs=None, mb=None, aliases={}):
    return pl.pallas_call(
        kernel,
        out_shape=out,
        in_specs=[ANY] * len(hbm) + [VMEM] * len(vmem) + [ANY] * len(deps),
        out_specs=out_specs or (VMEM,) * len(out),
        scratch_shapes=scratch,
        compiler_params=pltpu.CompilerParams(vmem_limit_bytes=mib * 2**20),
        input_output_aliases=aliases,
        cost_estimate=mb and pl.CostEstimate(flops=0, bytes_accessed=mb * 2**20, transcendentals=0),
        name=name,
    )(*[in_hbm(v) for v in hbm], *[in_vmem(v) for v in vmem], *deps)


def split(x):
    hi = x.astype(BF16)
    return hi, (x - hi.astype(F32)).astype(BF16)


def dot(a, b):
    return jnp.dot(a, b, preferred_element_type=F32)


def pair_of(b):
    bh, bl = split(b)
    return jnp.concatenate([bh, bl], axis=1)


def lhs_of(*blocks):
    parts = [split(b) for b in blocks]
    return jnp.concatenate([hi for hi, _ in parts] + [lo for _, lo in parts], axis=0)


def dot3(lhs, both):
    n = lhs.shape[0] // 2
    prod = dot(lhs, both)
    return prod[:n, :W] + (prod[:n, W:] + prod[n:, :W])


def core():
    return lax.rem(lax.axis_index("col"), 2)


def chip():
    return lax.axis_index("col") // 2


def side():
    return lax.rem(core() + chip() + odd_row(), 2)


def odd_row():
    return lax.rem(lax.axis_index("row"), 2)


def lane_group(shape):
    return lax.broadcasted_iota(jnp.int32, shape, 1) // 32


def on_chain(kernel):
    @functools.wraps(kernel)
    def gated(*refs):
        @pl.when(lax.axis_index("row") < 2)
        def _():
            kernel(*refs)

    return gated


def packed(rows):
    group = lane_group(rows[0].shape)
    high, odd = group >= 2, group % 2 == 1
    out = list(rows)
    for g in range(2):
        a, b = out[g], out[g + 2]
        turned = pltpu.roll(jnp.where(high, a, b), 64, 1)
        out[g], out[g + 2] = jnp.where(high, turned, a), jnp.where(high, b, turned)
    for g in (0, 2):
        a, b = out[g], out[g + 1]
        out[g], out[g + 1] = jnp.where(odd, pltpu.roll(b, 32, 1), a), jnp.where(odd, b, pltpu.roll(a, 96, 1))
    return out


def unpack(p):
    group = lane_group(p.shape)
    turned = [p] + [pltpu.roll(p, 32 * n, 1) for n in (1, 2, 3)]
    out = []
    for g in range(4):
        m = p
        for n in (1, 2, 3):
            m = jnp.where(group == (g + n) % 4, turned[n], m)
        out.append(m)
    return jnp.concatenate(out, axis=0)


@on_chain
def start_kernel(p_ref, send_ref, keep_ref, p_buf, q_buf, sem):
    h = side()
    copies = [
        pltpu.make_async_copy(p_ref.at[0, pl.ds(PACK * g, PACK), :], p_buf.at[g], sem.at[g]) for g in range(4)
    ]
    for c in copies:
        c.start()
    for c in copies:
        c.wait()
    for b, block in enumerate(packed([p_buf[g] for g in range(4)])):
        q_buf[b] = block
    for r in range(2):
        keep_ref[r] = q_buf[2 * r + h]
        send_ref[r] = q_buf[2 * r + 1 - h]


def start(partials):
    return call(
        start_kernel,
        "start",
        (vm((2, PACK, W)), vm((2, PACK, W))),
        hbm=(partials,),
        scratch=[
            pltpu.VMEM((4, PACK, W), F32),
            pltpu.VMEM((4, PACK, W), F32),
            pltpu.SemaphoreType.DMA((4,)),
        ],
    )


@on_chain
def tile_kernel(panel_ref, dep_ref, out_ref, buf, sem):
    copy = pltpu.make_async_copy(panel_ref.at[0], buf, sem.at[0])
    copy.start()
    copy.wait()
    out_ref[:NB] = buf[pl.ds(0, NB, stride=2), :]


def first_tile(panel, dep):
    return call(
        tile_kernel,
        "tile",
        (vm((NB + PACK, W)),),
        hbm=(panel,),
        deps=(dep,),
        scratch=[pltpu.VMEM((2 * NB, W), F32), pltpu.SemaphoreType.DMA((1,))],
        mb=8,
    )[0]


@on_chain
def prep_kernel(inv_ref, rhs_ref, dep_ref, inv_out, rhs_out, r_buf, q_buf, sem):
    one = pltpu.make_async_copy(rhs_ref, r_buf, sem.at[0])
    two = pltpu.make_async_copy(inv_ref, inv_out, sem.at[1])
    one.start()
    two.start()
    one.wait()
    b = 2 * odd_row() + side()
    for k in range(2):
        for at, block in enumerate(packed([r_buf[k, PACK * g : PACK * (g + 1)] for g in range(4)])):
            q_buf[at] = block
        rhs_out[k] = q_buf[b]
    two.wait()


def prep(inverse, rhs, dep):
    return call(
        prep_kernel,
        "prep",
        (vm((2, W, NB)), vm((2, PACK, W))),
        hbm=(inverse, rhs),
        deps=(dep,),
        scratch=[
            pltpu.VMEM((2, NB, W), F32),
            pltpu.VMEM((4, PACK, W), F32),
            pltpu.SemaphoreType.DMA((2,)),
        ],
        mb=8,
    )


@on_chain
def add_kernel(a_ref, b_ref, _, mine_ref, other_ref, tile_ref):
    r = odd_row()
    mine_ref[...] = a_ref[r] + b_ref[r]
    other = a_ref[1 - r] + b_ref[1 - r]
    other_ref[...] = other
    tile_ref[NB:] = other


def add(a, b, tile):
    return call(add_kernel, "add", (PACKED, PACKED, vm(tile.shape)), vmem=(a, b, tile), aliases={2: 2})


@on_chain
def order_kernel(mine_ref, got_ref, _, even_ref, same_ref):
    r = odd_row()

    @pl.when(r == 0)
    def _():
        even_ref[...] = mine_ref[...]

    @pl.when(r == 1)
    def _():
        even_ref[...] = got_ref[...]


def order(mine, got, rhs):
    return call(order_kernel, "order", (PACKED, vm(rhs.shape)), vmem=(mine, got, rhs), aliases={2: 1})


@on_chain
def odd_kernel(own_ref, got_ref, dep0, dep1, dep2, dep3, out_ref):
    r = odd_row()

    @pl.when(r == 1)
    def _():
        out_ref[...] = own_ref[:NB]

    @pl.when(r == 0)
    def _():
        out_ref[...] = got_ref[:NB]


def odd_tile(own, got, deps):
    return call(odd_kernel, "odd", (vm((NB, W)),), vmem=(own, got), deps=deps)[0]


@on_chain
def rows_kernel(own_ref, got_ref, out_ref):
    for k in range(2):
        out_ref[k] = lhs_of(own_ref[k], got_ref[k])


def inverse_rows(own, got):
    return call(rows_kernel, "rows", (vm((2, 4 * W, NB), BF16),), vmem=(own, got), mib=8)[0]


def times_tile(out, tile_ref, y):
    both = pair_of(y)
    group = lane_group(out.shape)
    for g in range(4):
        u = dot3(lhs_of(tile_ref[pl.ds(PACK * g, PACK), :]), both)
        out = jnp.where(group == g, out + u, out)
    return out


@on_chain
def first_kernel(rhs_ref, a, b, c, d, inv_ref, y_ref):
    total = (a[...] + b[...]) + (c[...] + d[...])
    y = dot3(inv_ref[0], pair_of(unpack(rhs_ref[0] - total)))
    y_ref[0] = y[:W]
    y_ref[1] = y[W:]


def first(rhs, sums, inv):
    return call(first_kernel, "first", (vm((2, W, W)),), vmem=(rhs, *sums, inv), mib=8)[0]


@on_chain
def half_kernel(mine_ref, got_ref, y_ref, tile_ref, out_ref):
    odd = odd_row() == 1
    y = jnp.where(odd, y_ref[0], y_ref[1])
    out_ref[...] = times_tile(jnp.where(odd, mine_ref[...], got_ref[NB:]), tile_ref, y)


def half(mine, got, y, tile):
    return call(half_kernel, "half", (PACKED,), vmem=(mine, got, y, tile), mib=8)[0]


@on_chain
def rest_kernel(u_ref, y_ref, tile_ref, out_ref):
    y = jnp.where(odd_row() == 1, y_ref[1], y_ref[0])
    out_ref[...] = times_tile(u_ref[...], tile_ref, y)


def rest(u, y, tile):
    return call(rest_kernel, "rest", (PACKED,), vmem=(u, y, tile), mib=8)[0]


@on_chain
def second_kernel(rhs_ref, a, b, c, d, inv_ref, y_ref, dep_ref, out_ref):
    total = (a[...] + b[...]) + (c[...] + d[...])
    y = dot3(inv_ref[1], pair_of(unpack(rhs_ref[1] - total)))
    group = lane_group((W, W))
    own = jnp.where(group < 2, y_ref[0], y[:W])
    got = jnp.where(group < 2, y_ref[1], y[W:])
    out_ref[...] = jnp.where(group % 2 == core(), own, got)


def second(rhs, sums, inv, y0, dep):
    return call(
        second_kernel, "second", (vm((W, W)),), vmem=(rhs, *sums, inv, y0), deps=(dep,), mib=8
    )[0]


def choose_kernel(a, b, c, d, out_ref):
    x = lax.axis_index("row") // NZ
    for m, got in zip(X_STEPS, (a, b, c, d)):

        @pl.when(x == m)
        def _():
            out_ref[...] = got[...]


def choose(got):
    return call(choose_kernel, "choose", (vm((W, W)),), vmem=got)[0]


GROUP = 4


def parts_kernel(group, panel_ref, p_ref, dep_ref, hi_ref, lo_ref, part_ref, buf, sem):
    bring = pltpu.make_async_copy(p_ref.at[pl.ds(group * GROUP, GROUP)], part_ref, sem.at[GROUP])
    copies = [
        pltpu.make_async_copy(panel_ref.at[group * GROUP + l], buf.at[l, pl.ds(0, 2 * NB), :], sem.at[l])
        for l in range(GROUP)
    ]
    for c in copies:
        c.start()
    bring.start()
    for l in range(GROUP):
        copies[l].wait()
        for k in range(2):
            hi, lo = split(buf[l, pl.ds(k, NB, stride=2), :])
            hi_ref[l, :, k * W : (k + 1) * W] = hi
            lo_ref[l, :, k * W : (k + 1) * W] = lo
    bring.wait()


def parts(group, panel, partials, dep):
    out = vm((GROUP, NB, 2 * W), BF16)
    return call(
        functools.partial(parts_kernel, group),
        "parts",
        (out, out, vm((GROUP, NB, W))),
        hbm=(panel, partials),
        deps=(dep,),
        scratch=[pltpu.VMEM((GROUP, 2 * NB + 8, W), F32), pltpu.SemaphoreType.DMA((GROUP + 1,))],
        mib=6,
        mb=12,
    )


def deal_kernel(a, b, c, d, keep_ref, send_ref, sides):
    z = lax.rem(lax.axis_index("row"), NZ)
    for at, (from_0, from_1) in enumerate(((a, d), (b, a), (d, c), (c, b))):

        @pl.when(z == at)
        def _():
            sides[0] = from_0[...]
            sides[1] = from_1[...]

    left, right = sides[0], sides[1]
    group = lane_group((W, W))

    def lanes(parts):
        (p, i), (q, j), (r, k), (t, n) = parts
        turn = lambda v, shift: pltpu.roll(v, shift, 1) if shift else v
        low = jnp.where(group == 0, turn(p, i), turn(q, j))
        return jnp.where(group < 2, low, jnp.where(group == 2, turn(r, k), turn(t, n)))

    zero = lanes(((left, 0), (left, 96), (right, 64), (right, 32)))
    one = lanes(((left, 96), (left, 64), (right, 32), (right, 0)))
    h = core()
    keep_ref[...] = jnp.where(h == 0, zero, one)
    send_ref[...] = jnp.where(h == 0, one, zero)


def deal(got):
    return call(
        deal_kernel, "deal", (vm((W, W)), vm((W, W))), vmem=got, scratch=[pltpu.VMEM((2, W, W), F32)]
    )


def update_kernel(keep_ref, got_ref, ph0, pl0, part0, ph1, pl1, part1, out_ref, solved_ref, buf, y_buf, sem):
    row = lax.axis_index("row")
    x, z = row // NZ, lax.rem(row, NZ)
    way = core() + chip() + jnp.where(x == 0, 0, 1)
    left = lax.rem(way + jnp.where(z == 0, 0, 1), 2)
    right = lax.rem(way + jnp.where(z == 1, 0, 1) + 1, 2)
    group = lane_group((W, W))
    mine = group == jnp.where(group < 2, left, 2 + right)
    keep, got = keep_ref[...], got_ref[...]
    even = group % 2 == 0

    def block(k):
        if k == 0:
            spread = lambda v: jnp.where(even, v, pltpu.roll(v, 32, 1))
        else:
            spread = lambda v: jnp.where(even, pltpu.roll(v, 96, 1), v)
        return jnp.where(mine, spread(keep), spread(got))

    y0, y1 = block(0), block(1)
    y_buf[0] = y0
    y_buf[1] = y1
    solved = pltpu.make_async_copy(y_buf, solved_ref, sem.at[9])
    solved.start()
    head = pair_of(jnp.concatenate([jnp.where(row > 0, y0, 0.0), jnp.where(row > 1, y1, 0.0)], axis=0))
    rest = pair_of(jnp.concatenate([y0, y1], axis=0))

    pieces = [(l, 0, NB) for l in range(7)] + [(7, 0, NB // 2), (7, NB // 2, NB // 2)]
    copies = []
    for n, (l, at, size) in enumerate(pieces):
        hi, lo, part = ((ph0, pl0, part0), (ph1, pl1, part1))[l // GROUP]
        w = head if l == 0 else rest
        rows = pl.ds(at, size)
        prod = dot(hi[l % GROUP, rows, :], w)
        low = dot(lo[l % GROUP, rows, :], w[:, :W])
        buf[l, rows, :] = part[l % GROUP, rows, :] + (prod[:, :W] + (prod[:, W:] + low))
        copies.append(pltpu.make_async_copy(buf.at[l, rows, :], out_ref.at[l, rows, :], sem.at[n]))
        copies[-1].start()
    for c in copies:
        c.wait()
    solved.wait()


def update(keep, got, parts0, parts1):
    return call(
        update_kernel,
        "update",
        (jax.ShapeDtypeStruct((8, NB, W), F32), jax.ShapeDtypeStruct((2, W, W), F32)),
        vmem=(keep, got, *parts0, *parts1),
        out_specs=(ANY, ANY),
        scratch=[
            pltpu.VMEM((8, NB, W), F32),
            pltpu.VMEM((2, W, W), F32),
            pltpu.SemaphoreType.DMA((10,)),
        ],
        mib=10,
    )


def exchange(x, row_mask, col_mask):
    pairs = []
    for r in range(16):
        for c in range(8):
            chain = r < 2
            pairs.append((r * 8 + c, (r ^ row_mask) * 8 + (c ^ col_mask) if chain else r * 8 + (c ^ 1)))
    return lax.ppermute(x, ("row", "col"), pairs)


def swap(x):
    return exchange(x, 0, 1)


def chips(x):
    return [x] + [exchange(x, 0, mask) for mask in (7, 3, 4)]


def step(x, place):
    pairs = [(r * 8 + c, place(r // NZ, r % NZ) * 8 + (c ^ 1)) for r in range(16) for c in range(8)]
    return lax.ppermute(x, ("row", "col"), pairs)


def around(cycle):
    return lambda x, z: cycle.get(x * NZ + z, x * NZ + z)


def along_x(y):
    cycles = {1: {0: 1, 1: 0}, 2: {0: 2, 2: 1, 1: 0}, 3: {0: 3, 3: 0}}
    place = lambda m: lambda x, z: (cycles[m].get(x, x) if z < 2 else x) * NZ + z
    return [y] + [step(y, place(m)) for m in X_STEPS[1:]]


def along_z(y):
    cycles = ({0: 2, 1: 0, 2: 1}, {0: 3, 3: 0, 1: 2, 2: 1}, {0: 1, 1: 3, 3: 0})
    place = lambda cycle: lambda x, z: x * NZ + cycle.get(z, z)
    return [y] + [step(y, place(cycle)) for cycle in cycles[::-1]]


def per_device(partials, panel, inverse, rhs):
    inv_got = swap(inverse)
    partials = partials.reshape(8, NB, W)
    panel = panel.reshape(8, 2 * NB, W)
    send, keep = start(partials)
    tile = first_tile(panel, send)
    up = around({0: 1, 1: NZ + 1, NZ + 1: NZ, NZ: 0})
    down = around({1: 0, 0: NZ, NZ: NZ + 1, NZ + 1: 1})
    mine, other, tile = add(keep, swap(send), tile)
    tile_odd = step(tile, down)
    inv, rhs = prep(inverse, rhs, mine)
    even, rhs = order(mine, step(other, up), rhs)
    parts0 = parts(0, panel, partials, even)
    inv = inverse_rows(inv, inv_got)
    sums = chips(even)
    tile = odd_tile(tile, tile_odd, (*sums[1:], parts0[0]))
    y0 = first(rhs, sums, inv)
    u = rest(half(mine, tile_odd, y0, tile), y0, swap(tile))
    parts1 = parts(1, panel, partials, u)
    y = second(rhs, chips(u), inv, y0, parts1[0])
    keep, send = deal(along_z(choose(along_x(y))))
    new, solved = update(keep, swap(send), parts0, parts1)
    return new[None, :, None], solved


def solution(mesh):
    return jax.shard_map(
        per_device,
        mesh=mesh,
        in_specs=(
            P("col", None, "row", None, None),
            P(None, "row", None, None, "col"),
            P(None, "col", None),
            P(),
        ),
        out_specs=(P("col", None, "row", None, None), P(None, "col", None)),
        check_vma=False,
    )
```
